512 devices in a mesh: kvp: 64 (over y, x, core), tp: 8 (over z).
Axes of the slice: x: 4, y: 8, z: 8, core: 2. Of those that a mesh axis runs over, the one named last changes fastest.
Arguments:
- queries: bfloat16 [2, 16, 128, 128], P(None, None, 'tp', 'kvp'), may hold values from -8 to 8
- fresh_kv: bfloat16 [2, 16, 2, 8, 128], P(None, None, None, 'tp', 'kvp'), may hold values from -8 to 8
- kv_cache: bfloat16 [4096, 2, 8, 1024], P('kvp', None, None, 'tp'), may hold values from -8 to 8
- page_owner: int32 [4096], replicated, may hold values from 0 to 63, as said below
- context_pages: int32 [16], replicated, may hold values from 1 to 512, 4096 in all
- residual: bfloat16 [32, 16384], P(None, ('kvp', 'tp')), may hold values from -8 to 8
- out_proj: bfloat16 [16384, 16384], P('tp', 'kvp'), may hold values from -0.046875 to 0.046875
- norm_gain: bfloat16 [16384], P(('kvp', 'tp')), may hold values from 0.099609375 to 1.8984375
- gate_weight: bfloat16 [64, 256, 26624], P(None, 'tp', 'kvp'), may hold values from -0.046875 to 0.046875
- up_weight: bfloat16 [64, 256, 26624], P(None, 'tp', 'kvp'), may hold values from -0.046875 to 0.046875
Outputs:
- regrouped: bfloat16 [4096, 2, 8, 1024], P('kvp', None, None, 'tp')
- stream: bfloat16 [32, 16384], P(None, ('kvp', 'tp'))
- hidden: bfloat16 [32, 26624], P(None, ('kvp', 'tp'))
The draws below stay inside these ranges and needn't reach their ends.
Inputs may be any that keep to these rules, and one draw needn't show every extreme that they name: `page_owner`: each device's contiguous block of 64 pages names every owner exactly 1 times.
All inputs are finite; a program needn't handle non-finite values.
Results may differ from the reference program's by a relative error of at most 0.035.
Values may be sent and summed in bfloat16 or wider, within the bound.
No kernel may reach another device: no remote copies, remote signals or barrier semaphores. Data moves between devices by JAX's collectives and lax.ppermute only.
A program may use at most 64 MiB of HBM per device.

```python
import math
import jax
import jax.numpy as jnp
import numpy as np
from jax import lax

D = 16384
HEADS = 128
KVH = 8
HD = 128
FF = 26624
PAGE = 8
STEPS = 2
ROWS = 16
PAGES_PEER = 1
PAGES_DEV = 64
PAGES = 4096
MOST = 512
BATCH = 32
N_KVP = 64


def draw_queries(key, part):
    key = jax.random.fold_in(key, 11)
    noise_key = jax.random.fold_in(key, 0)
    noise = jax.random.truncated_normal(noise_key, -4.0, 4.0, (STEPS, ROWS, HEADS, HD), jnp.float32)
    drawn = noise
    return drawn.astype(jnp.bfloat16)


def draw_kv_cache(key, part):
    key = jax.random.fold_in(key, 12)
    noise_key = jax.random.fold_in(key, 0)
    noise = jax.random.truncated_normal(noise_key, -4.0, 4.0, (PAGES, 2, PAGE, KVH, HD), jnp.float32)
    drawn = noise
    return drawn.reshape(PAGES, 2, PAGE, KVH * HD).astype(jnp.bfloat16)


def draw_fresh_kv(key, part):
    key = jax.random.fold_in(key, 13)
    noise_key = jax.random.fold_in(key, 0)
    noise = jax.random.truncated_normal(noise_key, -4.0, 4.0, (STEPS, ROWS, 2, KVH, HD), jnp.float32)
    drawn = noise
    return drawn.astype(jnp.bfloat16)


def draw_page_owner(key, part):
    key = jax.random.fold_in(key, 14)
    blocks = PAGES // PAGES_DEV
    block_keys = jax.random.split(key, blocks)
    shuffled = jax.vmap(lambda block_key: jax.random.permutation(block_key, PAGES_DEV))(block_keys)
    return (shuffled // PAGES_PEER).reshape(PAGES).astype(jnp.int32)


def draw_residual(key, part):
    key = jax.random.fold_in(key, 15)
    noise_key, row_key = jax.random.split(key, 2)
    position = jnp.arange(D, dtype=jnp.float32) / D
    noise = jax.random.truncated_normal(noise_key, -6.0, 6.0, (BATCH, D), jnp.float32)
    row_scale = jnp.exp(jax.random.uniform(row_key, (BATCH, 1), minval=math.log(0.01), maxval=math.log(0.1)))
    column_scale = 10.0 ** position
    drawn = noise * row_scale * column_scale[None, :]
    return drawn.astype(jnp.bfloat16)


def level_of(own_key, shape, cuts, smallest, high):
    factor_of = 1.0
    for dim, shards_of in cuts:
        draws = jax.random.uniform(jax.random.fold_in(jax.random.fold_in(own_key, 6), dim), (shards_of,), jnp.float32, smallest / len(cuts), high / len(cuts))
        factor_of = factor_of * jnp.repeat(jnp.exp(draws), shape[dim] // shards_of).reshape((-1,) + (1,) * (len(shape) - 1 - dim))
    return factor_of


def length_profile(number_of, total, reach, lean):
    loads = [(1 << 20) // math.isqrt(grade ** lean) + 1 for grade in range(2, number_of + 1)]
    spare, counts = total - reach - (number_of - 1), [1] * (number_of - 1)
    while spare > 0:
        movable = [i for i in range(number_of - 1) if counts[i] < reach]
        pool, left = sum([loads[i] for i in movable]), spare
        for i in movable:
            addition = min(reach - counts[i], max(1, left * loads[i] // pool), spare)
            counts[i] = counts[i] + addition
            spare = spare - addition
    return np.array([reach] + counts)


def ragged_sizes(rng, count, total, most, slope):
    if count == 2:
        one = jax.random.randint(rng, (), max(1, total - most), min(most, total - 1) + 1)
        return jnp.stack([one, total - one])
    tallies = jnp.asarray(length_profile(count, total, most, slope), jnp.int32)
    pairs = (count - 1) // 2
    source_of, taker = tallies[1:1 + 2 * pairs:2], tallies[2:2 + 2 * pairs:2]
    slack = jnp.minimum(source_of - 1, most - taker)
    shifted = jax.random.randint(jax.random.fold_in(rng, 1), (pairs,), 0, 1 << 20) % (slack + 1)
    tallies = tallies.at[1:1 + 2 * pairs:2].set(source_of - shifted).at[2:2 + 2 * pairs:2].set(taker + shifted)
    return tallies[jax.random.permutation(jax.random.fold_in(rng, 2), count)]


def gaussian(rng, shape, width, bound, cuts=(), held_as=jnp.bfloat16):
    entries = jax.random.normal(rng, shape, jnp.float32) * width
    if len(cuts) > 0:
        entries = level_of(rng, shape, cuts, -0.22, 0.18) * entries
    return jnp.clip(entries, min=-bound, max=bound).astype(held_as)


def setup_inputs(seed: int = 0) -> dict:
    key_list = jax.random.split(jax.random.key(seed), 11)
    return {
        "queries": draw_queries(jax.random.fold_in(key_list[10], 71), 0),
        "fresh_kv": draw_fresh_kv(jax.random.fold_in(key_list[10], 71), 0),
        "kv_cache": draw_kv_cache(jax.random.fold_in(key_list[10], 71), 0),
        "page_owner": draw_page_owner(jax.random.fold_in(key_list[10], 71), 0),
        "context_pages": ragged_sizes(key_list[4], ROWS, PAGES, MOST, 2).astype(jnp.int32),
        "residual": draw_residual(jax.random.fold_in(key_list[10], 71), 0),
        "out_proj": gaussian(key_list[6], (HEADS * HD, D), (HEADS * HD) ** -0.5, 0.046875, ((0, 8), (1, 64))),
        "norm_gain": jnp.clip(1.0 + 0.18 * jax.random.normal(key_list[7], (D,), jnp.float32), 0.099609375, 1.8984375).astype(jnp.bfloat16),
        "gate_weight": gaussian(key_list[8], (N_KVP, D // N_KVP, FF), D ** -0.5, 0.046875, ((1, 8), (2, 64))),
        "up_weight": gaussian(key_list[9], (N_KVP, D // N_KVP, FF), D ** -0.5, 0.046875, ((1, 8), (2, 64))),
    }


def reference(queries, fresh_kv, kv_cache, page_owner, context_pages, residual, out_proj, norm_gain, gate_weight, up_weight):
    group_size = HEADS // KVH
    score_scale = HD ** (-0.5)
    highest = lax.Precision.HIGHEST
    ordering = jnp.argsort(page_owner, stable=True).astype(jnp.int32)
    regrouped = jnp.take(kv_cache, ordering, axis=0)
    starts = jnp.cumsum(context_pages) - context_pages
    page_ids = jnp.arange(PAGES, dtype=jnp.int32)
    row_of = (lax.optimization_barrier(jnp.sum((starts[None, :] <= page_ids[:, None]).astype(jnp.int32), axis=1)) - 1).astype(jnp.int32)
    cache = kv_cache.astype(jnp.float32).reshape(PAGES, 2, PAGE, KVH, HD)
    query_all = queries.astype(jnp.float32).reshape(STEPS, ROWS, KVH, group_size, HD)
    fresh = fresh_kv.astype(jnp.float32)
    causal = jnp.arange(STEPS, dtype=jnp.int32)[:, None] >= jnp.arange(STEPS, dtype=jnp.int32)[None, :]

    def one_head(head):
        query_head = jnp.take(query_all, head, axis=2)
        page_keys = jnp.take(cache[:, 0], head, axis=2)
        page_values = jnp.take(cache[:, 1], head, axis=2)
        fresh_keys = jnp.take(fresh[:, :, 0], head, axis=2)
        fresh_values = jnp.take(fresh[:, :, 1], head, axis=2)
        query_pages = jnp.take(query_head, row_of, axis=1)
        cache_scores = jnp.einsum('spgd,ptd->psgt', query_pages, page_keys, precision=highest) * score_scale
        fresh_scores = jnp.einsum('srgd,urd->rsgu', query_head, fresh_keys, precision=highest) * score_scale
        fresh_scores = jnp.where(causal[None, :, None, :], fresh_scores, -jnp.inf)
        page_peak = lax.optimization_barrier(jnp.max(cache_scores, axis=3))
        peak = jnp.maximum(jax.ops.segment_max(page_peak, row_of, num_segments=ROWS), lax.optimization_barrier(jnp.max(fresh_scores, axis=3)))
        cache_weights = jnp.exp(cache_scores - jnp.take(peak, row_of, axis=0)[..., None])
        fresh_weights = jnp.exp(fresh_scores - peak[..., None])
        denominator = jax.ops.segment_sum(lax.optimization_barrier(jnp.sum(cache_weights, axis=3)), row_of, num_segments=ROWS) + lax.optimization_barrier(jnp.sum(fresh_weights, axis=3))
        cache_rounded = lax.optimization_barrier(cache_weights.astype(jnp.bfloat16)).astype(jnp.float32)
        fresh_rounded = lax.optimization_barrier(fresh_weights.astype(jnp.bfloat16)).astype(jnp.float32)
        page_terms = jnp.einsum('psgt,ptd->psgd', cache_rounded, page_values, precision=highest)
        numerator = jax.ops.segment_sum(page_terms, row_of, num_segments=ROWS)
        numerator = numerator + jnp.einsum('rsgu,urd->rsgd', fresh_rounded, fresh_values, precision=highest)
        return (numerator / denominator[..., None]).astype(jnp.bfloat16)
    per_head = lax.map(one_head, jnp.arange(KVH, dtype=jnp.int32))
    attended = per_head.transpose(2, 1, 0, 3, 4).reshape(STEPS * ROWS, HEADS * HD)
    projected = jnp.dot(attended, out_proj, preferred_element_type=jnp.float32)
    stream = (residual.astype(jnp.float32) + projected).astype(jnp.bfloat16)
    widened = stream.astype(jnp.float32)
    inverse = lax.rsqrt(lax.optimization_barrier(jnp.sum(widened * widened, axis=1)) / D + 1e-05)
    scaled = (widened * norm_gain.astype(jnp.float32)[None, :]).astype(jnp.bfloat16)
    gated = jnp.dot(scaled, gate_weight.reshape(D, FF), preferred_element_type=jnp.float32) * inverse[:, None]
    lifted = jnp.dot(scaled, up_weight.reshape(D, FF), preferred_element_type=jnp.float32) * inverse[:, None]
    hidden = (jax.nn.silu(gated) * lifted).astype(jnp.bfloat16)
    return (regrouped, stream, hidden)
```

```python
import jax
import jax.numpy as jnp
from jax import lax
from jax.experimental import pallas as pl
from jax.experimental.pallas import tpu as pltpu
from jax.sharding import PartitionSpec as P

D = 16384
HEADS = 128
KVH = 8
HD = 128
STEPS = 2
ROWS = 16
BATCH = STEPS * ROWS

negative = -1e30
epsilon = 1e-05
bf16 = jnp.bfloat16
f32 = jnp.float32
VMEM = pl.BlockSpec(memory_space=pltpu.VMEM)
SMEM = pl.BlockSpec(memory_space=pltpu.SMEM)
PARAMS = pltpu.CompilerParams(vmem_limit_bytes=48 * 1024 * 1024)


def call(body, name, out_shape, in_specs, *args, scratch=()):
    multiple = isinstance(out_shape, (tuple, list))
    return pl.pallas_call(
        body,
        out_shape=out_shape,
        in_specs=in_specs,
        out_specs=[VMEM] * len(out_shape) if multiple else VMEM,
        scratch_shapes=scratch,
        compiler_params=PARAMS,
        name=name,
    )(*args)


def to_owner_order(owner, pages, out):
    base = lax.axis_index("kvp") * pages.shape[0]

    def one(c, carry):
        out[owner[base + c]] = pages[c]
        return carry

    lax.fori_loop(0, pages.shape[0], one, 0, unroll=8)


def attention(context, gathered, pages, out):
    turned = gathered[...].astype(f32).T
    q = turned[: HEADS // KVH * BATCH].astype(bf16)
    fresh = turned[HEADS // KVH * BATCH :].astype(bf16)
    fresh_k, fresh_v = fresh[:BATCH], fresh[BATCH : 2 * BATCH]
    cache = pages[...].astype(f32)
    keys = cache[:, 0].reshape(-1, HD).astype(bf16)
    values = cache[:, 1].reshape(-1, HD).astype(bf16)
    combos, tokens = q.shape[0], keys.shape[0]
    me = lax.axis_index("kvp")
    scale = HD ** (-0.5)
    nt = (((1,), (1,)), ((), ()))
    scores = lax.dot_general(q, keys, nt, preferred_element_type=f32) * scale
    fresh_scores = lax.dot_general(q, fresh_k, nt, preferred_element_type=f32) * scale

    page_len = tokens // pages.shape[0]
    page = (
        lax.broadcasted_iota(jnp.int32, (1, tokens), 1) // page_len + me * pages.shape[0]
    )
    row = jnp.zeros((1, tokens), jnp.int32)
    end = jnp.int32(0)
    for r in range(ROWS - 1):
        end = end + context[r]
        row = row + (page >= end).astype(jnp.int32)
    combo = lax.broadcasted_iota(jnp.int32, (combos, 1), 0)
    combo_row = combo % ROWS
    combo_step = (combo // ROWS) % STEPS
    member = combo_row == row
    entry = lax.broadcasted_iota(jnp.int32, (1, BATCH), 1)
    fresh_member = (
        (combo_row == entry % ROWS) & (entry // ROWS <= combo_step) & (me == 0)
    )
    scores = jnp.where(member, scores, negative)
    fresh_scores = jnp.where(fresh_member, fresh_scores, negative)
    peak = jnp.maximum(
        jnp.max(scores, axis=1, keepdims=True), jnp.max(fresh_scores, axis=1, keepdims=True)
    )
    peak = peak.astype(bf16).astype(f32)
    weights = jnp.where(member, jnp.exp(scores - peak), 0.0)
    fresh_weights = jnp.where(fresh_member, jnp.exp(fresh_scores - peak), 0.0)
    total = jnp.sum(weights, axis=1, keepdims=True) + jnp.sum(
        fresh_weights, axis=1, keepdims=True
    )
    numerator = jnp.dot(
        weights.astype(bf16), values, preferred_element_type=f32
    ) + jnp.dot(fresh_weights.astype(bf16), fresh_v, preferred_element_type=f32)
    high = total.astype(bf16).astype(f32)
    lane = lax.broadcasted_iota(jnp.int32, (combos, HD), 1)
    stats = jnp.where(lane < 32, peak, jnp.where(lane < 64, high, total - high))
    peers = out.shape[0]
    out[...] = jnp.concatenate(
        [numerator.reshape(peers, -1, HD), stats.reshape(peers, -1, HD)], axis=1
    ).astype(bf16)


def merge(parts, out):
    x = parts[...].astype(f32)
    count = x.shape[1] // 2
    numerator, stats = x[:, :count], x[:, count:]
    peak = stats[:, :, 0:1]
    total = stats[:, :, 32:33] + stats[:, :, 64:65]
    top = jnp.max(peak, axis=0, keepdims=True)
    factor = jnp.exp(peak - top)
    denominator = jnp.sum(factor * total, axis=0)
    value = jnp.sum(factor * numerator, axis=0) / denominator
    out[...] = jnp.broadcast_to(value.astype(bf16)[None], out.shape)


def pack(x):
    return jnp.concatenate([x[8 * q : 8 * q + 8] for q in range(4)], axis=1)


def project(attended, weight, out):
    x = attended[...].astype(f32).reshape(-1, BATCH, HD).astype(bf16)
    flat = jnp.concatenate([x[h] for h in range(x.shape[0])], axis=1)
    acc = jnp.dot(flat, weight[...], preferred_element_type=f32)
    for j in range(out.shape[0]):
        out[j] = pack(acc[:, 32 * j : 32 * j + 32]).astype(bf16)


def add_residual(parts, residual, stream, sent):
    total = jnp.sum(parts[...].astype(f32), axis=0)
    value = (total + pack(residual[...].astype(f32))).astype(bf16)
    sent[...] = jnp.broadcast_to(value[None], sent.shape)
    wide = value.astype(f32)
    stream[...] = jnp.concatenate(
        [wide[:, 32 * q : 32 * q + 32] for q in range(4)], axis=0
    ).astype(bf16)


def feed_forward(columns, gain, gate_weight, up_weight, out):
    x = columns[...].astype(f32)
    square = jnp.sum(x * x, axis=0)
    square = jnp.concatenate(
        [jnp.sum(square[:, 32 * q : 32 * q + 32], axis=1, keepdims=True) for q in range(4)],
        axis=0,
    )
    scaled = (x * gain[...].astype(f32)).reshape(-1, 4, 8, HD)
    lane = lax.broadcasted_iota(jnp.int32, (scaled.shape[0], 8, HD), 2) // 32
    blocks = []
    for q in range(4):
        block = None
        for t in range(4):
            piece = scaled[:, t]
            if t != q:
                piece = pltpu.roll(piece, (t - q) * 32 % HD, 2)
            block = piece if block is None else jnp.where(lane == t, piece, block)
        blocks.append(block)
    rows = jnp.concatenate(blocks, axis=1).astype(bf16)
    flat = jnp.concatenate([rows[g] for g in range(rows.shape[0])], axis=1)
    width = gate_weight.shape[2]
    gate = jnp.dot(flat, gate_weight[...].reshape(-1, width), preferred_element_type=f32)
    up = jnp.dot(flat, up_weight[...].reshape(-1, width), preferred_element_type=f32)
    peers = out.shape[0]
    part = width // peers
    high = square.astype(bf16).astype(f32)
    tail = lax.broadcasted_iota(jnp.int32, (BATCH, 64 - part), 1)
    tail = jnp.where(tail == 0, high, jnp.where(tail == 1, square - high, 0.0))
    gap = jnp.zeros((BATCH, 64 - part), f32)
    for j in range(peers):
        out[j] = jnp.concatenate(
            [
                gate[:, part * j : part * j + part],
                gap,
                up[:, part * j : part * j + part],
                tail,
            ],
            axis=1,
        ).astype(bf16)


def activate(parts, out):
    total = jnp.sum(parts[...].astype(f32), axis=0)
    part = out.shape[1]
    square = total[:, 64 + part : 65 + part] + total[:, 65 + part : 66 + part]
    inverse = lax.rsqrt(square / D + epsilon)
    gated = total[:, :part] * inverse
    lifted = total[:, 64 : 64 + part] * inverse
    out[...] = (gated / (1.0 + jnp.exp(-gated)) * lifted).astype(bf16)


def exchange(x, axis):
    return lax.all_to_all(x, axis, split_axis=0, concat_axis=0, tiled=True)


def shards(
    queries,
    fresh_kv,
    kv_cache,
    page_owner,
    context_pages,
    residual,
    out_proj,
    norm_gain,
    gate_weight,
    up_weight,
):
    kvp = lax.axis_size("kvp")
    tp = lax.axis_size("tp")
    shape = jax.ShapeDtypeStruct
    combos = queries.shape[2] * BATCH

    q = queries.transpose(3, 2, 0, 1).reshape(2, combos)
    fresh = fresh_kv[:, :, :, 0].transpose(3, 2, 0, 1).reshape(2, 2 * BATCH)
    gain = jnp.tile(norm_gain, 4).reshape(2, 2 * BATCH)
    sent = jnp.concatenate([q, fresh, gain], axis=1)
    gathered = exchange(jnp.broadcast_to(sent[None], (kvp,) + sent.shape), "kvp")
    gain_rows = gathered[:, :, combos + 2 * BATCH :].reshape(kvp, 1, HD)

    outgoing = call(
        to_owner_order, "to_owner_order", shape(kv_cache.shape, bf16), [SMEM, VMEM], page_owner, kv_cache
    )
    parts = call(
        attention,
        "attention",
        shape((kvp, 2 * combos // kvp, HD), bf16),
        [SMEM, VMEM, VMEM],
        context_pages,
        gathered.reshape(2 * kvp, -1),
        kv_cache,
    )
    parts = exchange(parts, "kvp")
    piece = call(merge, "merge", shape((kvp, combos // kvp, HD), bf16), [VMEM], parts)
    attended = exchange(piece, "kvp")
    partial = call(
        project, "project", shape((tp, 8, HD), bf16), [VMEM, VMEM], attended, out_proj
    )
    partial, outgoing = lax.optimization_barrier((partial, outgoing))
    regrouped = exchange(outgoing, "kvp")
    summands = exchange(partial, "tp")
    stream, block = call(
        add_residual,
        "add_residual",
        [shape(residual.shape, bf16), shape((kvp, 8, HD), bf16)],
        [VMEM, VMEM],
        summands,
        residual,
    )
    columns = exchange(block, "kvp")
    lifted = call(
        feed_forward,
        "feed_forward",
        shape((tp, BATCH, HD), bf16),
        [VMEM] * 4,
        columns,
        gain_rows,
        gate_weight,
        up_weight,
    )
    lifted = exchange(lifted, "tp")
    hidden = call(
        activate, "activate", shape((BATCH, gate_weight.shape[2] // tp), bf16), [VMEM], lifted
    )
    return regrouped, stream, hidden


def solution(mesh):
    return jax.shard_map(
        shards,
        mesh=mesh,
        in_specs=(
            P(None, None, "tp", "kvp"),
            P(None, None, None, "tp", "kvp"),
            P("kvp", None, None, "tp"),
            P(),
            P(),
            P(None, ("kvp", "tp")),
            P("tp", "kvp"),
            P(("kvp", "tp")),
            P(None, "tp", "kvp"),
            P(None, "tp", "kvp"),
        ),
        out_specs=(P("kvp", None, None, "tp"), P(None, ("kvp", "tp")), P(None, ("kvp", "tp"))),
        check_vma=False,
    )
```

```python
import jax
import jax.numpy as jnp
from jax import lax
from jax.experimental import pallas as pl
from jax.experimental.pallas import tpu as pltpu
from jax.sharding import PartitionSpec as P

D = 16384
HEADS = 128
KVH = 8
HD = 128
STEPS = 2
ROWS = 16
BATCH = STEPS * ROWS

negative = -1e30
epsilon = 1e-05
bf16 = jnp.bfloat16
f32 = jnp.float32
VMEM = pl.BlockSpec(memory_space=pltpu.VMEM)
SMEM = pl.BlockSpec(memory_space=pltpu.SMEM)
PARAMS = pltpu.CompilerParams(vmem_limit_bytes=16 * 1024 * 1024)
HBM = pl.BlockSpec(memory_space=pltpu.HBM)


def call(body, name, out_shape, in_specs, *args, out_specs=None, scratch=()):
    if out_specs is None:
        out_specs = [VMEM] * len(out_shape) if isinstance(out_shape, list) else VMEM
    return pl.pallas_call(
        body,
        out_shape=out_shape,
        in_specs=in_specs,
        out_specs=out_specs,
        scratch_shapes=scratch,
        compiler_params=PARAMS,
        name=name,
    )(*args)


def pack_inputs(raw, out):
    heads = raw.shape[3]
    blocks = raw[...].astype(f32)
    rows = blocks[:, :ROWS].reshape(2 * BATCH, heads).astype(bf16)
    entry = lax.broadcasted_iota(jnp.int32, (2 * BATCH, heads * BATCH), 0)
    target = lax.broadcasted_iota(jnp.int32, (2 * BATCH, heads * BATCH), 1)
    head = lax.broadcasted_iota(jnp.int32, (heads, heads * BATCH), 0)
    lane = lax.broadcasted_iota(jnp.int32, (heads, heads * BATCH), 1)
    lines = []
    for d in range(2):
        place = (entry % 2 == d) & (entry // 2 == target % BATCH)
        spread = lax.dot_general(
            rows,
            jnp.where(place, 1.0, 0.0).astype(bf16),
            (((0,), (0,)), ((), ())),
            preferred_element_type=f32,
        )
        lines.append(
            jnp.sum(jnp.where(lane // BATCH == head, spread, 0.0), axis=0, keepdims=True)
        )
    q = jnp.concatenate(lines, axis=0)
    kv = [blocks[u, ROWS + w] for w in range(2) for u in range(STEPS)]
    g = blocks[0, ROWS + 2]
    g = jnp.concatenate([g[:1], g[1:]] * 2, axis=1)
    line = jnp.concatenate([q] + kv + [jnp.concatenate([g, g], axis=0)], axis=1)
    out[...] = jnp.broadcast_to(line.astype(bf16)[None], out.shape)


def prepare(context, owner, pages, residual, keys, values, row_of, ordered, packed):
    me = lax.axis_index("kvp")
    count, page_len = pages.shape[0], pages.shape[2]
    cache = pages[...].astype(f32)
    keys[...] = cache[:, 0].reshape(-1, HD).astype(bf16)
    values[...] = cache[:, 1].reshape(-1, HD).astype(bf16)
    page = lax.broadcasted_iota(jnp.int32, row_of.shape, 1) // page_len + me * count
    row = jnp.zeros(row_of.shape, jnp.int32)
    end = jnp.int32(0)
    for r in range(ROWS - 1):
        end = end + context[r]
        row = row + (page >= end).astype(jnp.int32)
    row_of[...] = row
    packed[...] = pack(residual[...].astype(f32))

    def one(c, carry):
        ordered[owner[me * count + c]] = pages[c].reshape(2 * page_len, HD)
        return carry

    lax.fori_loop(0, count, one, 0, unroll=8)


def attention(gathered, key_ref, value_ref, row_ref, out, gain_out):
    turned = gathered[...].astype(f32).T
    q = turned[: HEADS // KVH * BATCH].astype(bf16)
    fresh = turned[HEADS // KVH * BATCH :].astype(bf16)
    fresh_k, fresh_v = fresh[:BATCH], fresh[BATCH : 2 * BATCH]
    keys, values = key_ref[...], value_ref[...]
    combos, tokens = q.shape[0], keys.shape[0]
    peers = out.shape[0]
    tail = gathered[...][:, combos + 2 * BATCH :]
    take = lax.broadcasted_iota(jnp.int32, (peers, 2 * peers), 1) - 2 * lax.broadcasted_iota(
        jnp.int32, (peers, 2 * peers), 0
    )
    gain_out[...] = jnp.concatenate(
        [
            jnp.dot(
                jnp.where(take == k, 1.0, 0.0).astype(bf16), tail, preferred_element_type=f32
            )
            for k in range(2)
        ],
        axis=1,
    )
    me = lax.axis_index("kvp")
    scale = HD ** (-0.5)
    nt = (((1,), (1,)), ((), ()))
    scores = lax.dot_general(q, keys, nt, preferred_element_type=f32) * scale
    fresh_scores = lax.dot_general(q, fresh_k, nt, preferred_element_type=f32) * scale

    row = row_ref[...][:1]
    combo = lax.broadcasted_iota(jnp.int32, (combos, 1), 0)
    combo_row = combo % ROWS
    combo_step = (combo // ROWS) % STEPS
    member = combo_row == row
    entry = lax.broadcasted_iota(jnp.int32, (1, BATCH), 1)
    fresh_member = (
        (combo_row == entry % ROWS) & (entry // ROWS <= combo_step) & (me == 0)
    )
    scores = jnp.where(member, scores, negative)
    fresh_scores = jnp.where(fresh_member, fresh_scores, negative)
    peak = jnp.maximum(
        jnp.max(scores, axis=1, keepdims=True), jnp.max(fresh_scores, axis=1, keepdims=True)
    )
    peak = peak.astype(bf16).astype(f32)
    weights = jnp.where(member, jnp.exp(scores - peak), 0.0)
    fresh_weights = jnp.where(fresh_member, jnp.exp(fresh_scores - peak), 0.0)
    total = jnp.sum(weights, axis=1, keepdims=True) + jnp.sum(
        fresh_weights, axis=1, keepdims=True
    )
    numerator = jnp.dot(
        weights.astype(bf16), values, preferred_element_type=f32
    ) + jnp.dot(fresh_weights.astype(bf16), fresh_v, preferred_element_type=f32)
    high = total.astype(bf16).astype(f32)
    lane = lax.broadcasted_iota(jnp.int32, (combos, HD), 1)
    stats = jnp.where(lane < 32, peak, jnp.where(lane < 64, high, total - high))
    out[...] = jnp.concatenate(
        [numerator.reshape(peers, -1, HD), stats.reshape(peers, -1, HD)], axis=1
    ).astype(bf16)


def merge(parts, ordered, out):
    x = parts[...].astype(f32)
    count = x.shape[1] // 2
    numerator, stats = x[:, :count], x[:, count:]
    peak = stats[:, :, 0:1]
    total = stats[:, :, 32:33] + stats[:, :, 64:65]
    top = jnp.max(peak, axis=0, keepdims=True)
    factor = jnp.exp(peak - top)
    denominator = jnp.sum(factor * total, axis=0)
    value = jnp.sum(factor * numerator, axis=0) / denominator
    value = jnp.broadcast_to(value.astype(bf16)[None], (out.shape[0],) + value.shape)
    out[...] = jnp.concatenate([ordered[...], value], axis=1)


def pack(x):
    return jnp.concatenate([x[8 * q : 8 * q + 8] for q in range(4)], axis=1)


def project(attended, weight, out):
    x = attended[...][:, 16:].astype(f32).reshape(-1, BATCH, HD).astype(bf16)
    flat = jnp.concatenate([x[h] for h in range(x.shape[0])], axis=1)
    acc = jnp.dot(flat, weight[...], preferred_element_type=f32)
    for j in range(out.shape[0]):
        out[j] = pack(acc[:, 32 * j : 32 * j + 32]).astype(bf16)


def add_residual(parts, residual, own, sent):
    total = jnp.sum(parts[...].astype(f32), axis=0)
    value = (total + residual[...]).astype(bf16)
    own[...] = value.astype(f32)
    sent[...] = jnp.broadcast_to(value[None], sent.shape)


def feed_forward(
    columns, gain, gate_weight, up_weight, own, pages, out, stream, regrouped, staged, done
):
    wide = own[...]
    staged[...] = jnp.concatenate(
        [wide[:, 32 * q : 32 * q + 32] for q in range(4)], axis=0
    ).astype(bf16)
    copies = [
        pltpu.make_async_copy(pages.at[:, : regrouped.shape[1]], regrouped, done.at[0]),
        pltpu.make_async_copy(staged, stream, done.at[1]),
    ]
    for copy in copies:
        copy.start()
    x = columns[...].astype(f32)
    square = jnp.sum(x * x, axis=0)
    square = jnp.concatenate(
        [jnp.sum(square[:, 32 * q : 32 * q + 32], axis=1, keepdims=True) for q in range(4)],
        axis=0,
    )
    scaled = (x * gain[...][:, None, :]).reshape(-1, 4, 8, HD)
    lane = lax.broadcasted_iota(jnp.int32, (scaled.shape[0], 8, HD), 2) // 32
    blocks = []
    for q in range(4):
        block = None
        for t in range(4):
            piece = scaled[:, t]
            if t != q:
                piece = pltpu.roll(piece, (t - q) * 32 % HD, 2)
            block = piece if block is None else jnp.where(lane == t, piece, block)
        blocks.append(block)
    rows = jnp.concatenate(blocks, axis=1).astype(bf16)
    flat = jnp.concatenate([rows[g] for g in range(rows.shape[0])], axis=1)
    width = gate_weight.shape[2]
    gate = jnp.dot(flat, gate_weight[...].reshape(-1, width), preferred_element_type=f32)
    up = jnp.dot(flat, up_weight[...].reshape(-1, width), preferred_element_type=f32)
    peers = out.shape[0]
    part = width // peers
    high = square.astype(bf16).astype(f32)
    tail = lax.broadcasted_iota(jnp.int32, (BATCH, 64 - part), 1)
    tail = jnp.where(tail == 0, high, jnp.where(tail == 1, square - high, 0.0))
    gap = jnp.zeros((BATCH, 64 - part), f32)
    for j in range(peers):
        out[j] = jnp.concatenate(
            [
                gate[:, part * j : part * j + part],
                gap,
                up[:, part * j : part * j + part],
                tail,
            ],
            axis=1,
        ).astype(bf16)
    for copy in copies:
        copy.wait()


def activate(parts, out):
    total = jnp.sum(parts[...].astype(f32), axis=0)
    part = out.shape[1]
    square = total[:, 64 + part : 65 + part] + total[:, 65 + part : 66 + part]
    inverse = lax.rsqrt(square / D + epsilon)
    gated = total[:, :part] * inverse
    lifted = total[:, 64 : 64 + part] * inverse
    out[...] = (gated / (1.0 + jnp.exp(-gated)) * lifted).astype(bf16)


def exchange(x, axis):
    return lax.all_to_all(x, axis, split_axis=0, concat_axis=0, tiled=True)


def shards(
    queries,
    fresh_kv,
    kv_cache,
    page_owner,
    context_pages,
    residual,
    out_proj,
    norm_gain,
    gate_weight,
    up_weight,
):
    kvp = lax.axis_size("kvp")
    tp = lax.axis_size("tp")
    shape = jax.ShapeDtypeStruct
    combos = queries.shape[2] * BATCH

    count, page_len = kv_cache.shape[0], kv_cache.shape[2]
    tokens = count * page_len
    raw = jnp.concatenate(
        [
            queries.transpose(0, 1, 3, 2),
            fresh_kv[:, :, :, 0].transpose(0, 2, 3, 1),
            jnp.broadcast_to(norm_gain.reshape(1, 1, 2, ROWS), (STEPS, 1, 2, ROWS)),
        ],
        axis=1,
    )
    sent = call(
        pack_inputs,
        "pack_inputs",
        shape((kvp, 2, combos + 4 * BATCH), bf16),
        [VMEM],
        raw,
    )
    gathered = exchange(sent, "kvp")
    keys, values, row_of, ordered, packed = call(
        prepare,
        "prepare",
        [
            shape((tokens, HD), bf16),
            shape((tokens, HD), bf16),
            shape((8, tokens), jnp.int32),
            shape((count, 2 * page_len, HD), bf16),
            shape((8, HD), f32),
        ],
        [SMEM, SMEM, VMEM, VMEM],
        context_pages,
        page_owner,
        kv_cache,
        residual,
    )
    parts, gain_rows = call(
        attention,
        "attention",
        [shape((kvp, 2 * combos // kvp, HD), bf16), shape((kvp, HD), f32)],
        [VMEM] * 4,
        gathered.reshape(2 * kvp, -1),
        keys,
        values,
        row_of,
    )
    parts = exchange(parts, "kvp")
    piece = call(
        merge,
        "merge",
        shape((kvp, 2 * page_len + combos // kvp, HD), bf16),
        [VMEM] * 2,
        parts,
        ordered,
    )
    attended = exchange(piece, "kvp")
    partial = call(
        project, "project", shape((tp, 8, HD), bf16), [VMEM, VMEM], attended, out_proj
    )
    summands = exchange(partial, "tp")
    own, block = call(
        add_residual,
        "add_residual",
        [shape((8, HD), f32), shape((kvp, 8, HD), bf16)],
        [VMEM, VMEM],
        summands,
        packed,
    )
    columns = exchange(block, "kvp")
    lifted, stream, regrouped = call(
        feed_forward,
        "feed_forward",
        [
            shape((tp, BATCH, HD), bf16),
            shape(residual.shape, bf16),
            shape((count, 2 * page_len, HD), bf16),
        ],
        [VMEM] * 6,
        columns,
        gain_rows,
        gate_weight,
        up_weight,
        own,
        attended,
        out_specs=[VMEM, HBM, HBM],
        scratch=[pltpu.VMEM(residual.shape, bf16), pltpu.SemaphoreType.DMA((2,))],
    )
    lifted = exchange(lifted, "tp")
    hidden = call(
        activate, "activate", shape((BATCH, gate_weight.shape[2] // tp), bf16), [VMEM], lifted
    )
    return regrouped.reshape(kv_cache.shape), stream, hidden


def solution(mesh):
    return jax.shard_map(
        shards,
        mesh=mesh,
        in_specs=(
            P(None, None, "tp", "kvp"),
            P(None, None, None, "tp", "kvp"),
            P("kvp", None, None, "tp"),
            P(),
            P(),
            P(None, ("kvp", "tp")),
            P("tp", "kvp"),
            P(("kvp", "tp")),
            P(None, "tp", "kvp"),
            P(None, "tp", "kvp"),
        ),
        out_specs=(P("kvp", None, None, "tp"), P(None, ("kvp", "tp")), P(None, ("kvp", "tp"))),
        check_vma=False,
    )
```

```python
import jax
import jax.numpy as jnp
from jax import lax
from jax.experimental import pallas as pl
from jax.experimental.pallas import tpu as pltpu
from jax.sharding import PartitionSpec as P

D = 16384
HEADS = 128
KVH = 8
HD = 128
STEPS = 2
ROWS = 16
BATCH = STEPS * ROWS

negative = -1e30
epsilon = 1e-05
bf16 = jnp.bfloat16
f32 = jnp.float32
VMEM = pl.BlockSpec(memory_space=pltpu.VMEM)
SMEM = pl.BlockSpec(memory_space=pltpu.SMEM)
PARAMS = pltpu.CompilerParams(vmem_limit_bytes=16 * 1024 * 1024)
HBM = pl.BlockSpec(memory_space=pltpu.HBM)


def call(body, name, out_shape, in_specs, *args, out_specs=None, scratch=()):
    if out_specs is None:
        out_specs = [VMEM] * len(out_shape) if isinstance(out_shape, list) else VMEM
    return pl.pallas_call(
        body,
        out_shape=out_shape,
        in_specs=in_specs,
        out_specs=out_specs,
        scratch_shapes=scratch,
        compiler_params=PARAMS,
        name=name,
    )(*args)


def pack_inputs(raw, out):
    heads = raw.shape[3]
    blocks = raw[...].astype(f32)
    rows = blocks[:, :ROWS].reshape(2 * BATCH, heads).astype(bf16)
    entry = lax.broadcasted_iota(jnp.int32, (2 * BATCH, heads * BATCH), 0)
    target = lax.broadcasted_iota(jnp.int32, (2 * BATCH, heads * BATCH), 1)
    head = lax.broadcasted_iota(jnp.int32, (heads, heads * BATCH), 0)
    lane = lax.broadcasted_iota(jnp.int32, (heads, heads * BATCH), 1)
    lines = []
    for d in range(2):
        place = (entry % 2 == d) & (entry // 2 == target % BATCH)
        spread = lax.dot_general(
            rows,
            jnp.where(place, 1.0, 0.0).astype(bf16),
            (((0,), (0,)), ((), ())),
            preferred_element_type=f32,
        )
        lines.append(
            jnp.sum(jnp.where(lane // BATCH == head, spread, 0.0), axis=0, keepdims=True)
        )
    q = jnp.concatenate(lines, axis=0)
    kv = [blocks[u, ROWS + w] for w in range(2) for u in range(STEPS)]
    line = jnp.concatenate([q] + kv + [jnp.zeros((2, 2 * BATCH), f32)], axis=1)
    out[...] = jnp.broadcast_to(line.astype(bf16)[None], out.shape)


def prepare(
    context, owner, pages, residual, gain, keys, values, row_of, ordered, packed, gain_row
):
    me = lax.axis_index("kvp")
    count, page_len = pages.shape[0], pages.shape[2]
    cache = pages[...].astype(f32)
    keys[...] = cache[:, 0].reshape(-1, HD).astype(bf16)
    values[...] = cache[:, 1].reshape(-1, HD).astype(bf16)
    page = lax.broadcasted_iota(jnp.int32, row_of.shape, 1) // page_len + me * count
    row = jnp.zeros(row_of.shape, jnp.int32)
    end = jnp.int32(0)
    for r in range(ROWS - 1):
        end = end + context[r]
        row = row + (page >= end).astype(jnp.int32)
    row_of[...] = row
    packed[...] = pack(residual[...].astype(f32))
    line = gain[...].astype(f32)
    gain_row[...] = jnp.broadcast_to(
        jnp.concatenate([line] * 4, axis=1), gain_row.shape
    )

    def one(c, carry):
        ordered[owner[me * count + c]] = pages[c].reshape(2 * page_len, HD)
        return carry

    lax.fori_loop(0, count, one, 0, unroll=8)


def attention(gathered, key_ref, value_ref, row_ref, gain_row, out):
    turned = gathered[...].astype(f32).T
    q = turned[: HEADS // KVH * BATCH].astype(bf16)
    fresh = turned[HEADS // KVH * BATCH :].astype(bf16)
    fresh_k, fresh_v = fresh[:BATCH], fresh[BATCH : 2 * BATCH]
    keys, values = key_ref[...], value_ref[...]
    combos, tokens = q.shape[0], keys.shape[0]
    peers = out.shape[0]
    me = lax.axis_index("kvp")
    scale = HD ** (-0.5)
    nt = (((1,), (1,)), ((), ()))
    scores = lax.dot_general(q, keys, nt, preferred_element_type=f32) * scale
    fresh_scores = lax.dot_general(q, fresh_k, nt, preferred_element_type=f32) * scale

    row = row_ref[...][:1]
    combo = lax.broadcasted_iota(jnp.int32, (combos, 1), 0)
    combo_row = combo % ROWS
    combo_step = (combo // ROWS) % STEPS
    member = combo_row == row
    entry = lax.broadcasted_iota(jnp.int32, (1, BATCH), 1)
    fresh_member = (
        (combo_row == entry % ROWS) & (entry // ROWS <= combo_step) & (me == 0)
    )
    scores = jnp.where(member, scores, negative)
    fresh_scores = jnp.where(fresh_member, fresh_scores, negative)
    peak = jnp.maximum(
        jnp.max(scores, axis=1, keepdims=True), jnp.max(fresh_scores, axis=1, keepdims=True)
    )
    peak = peak.astype(bf16).astype(f32)
    weights = jnp.where(member, jnp.exp(scores - peak), 0.0)
    fresh_weights = jnp.where(fresh_member, jnp.exp(fresh_scores - peak), 0.0)
    total = jnp.sum(weights, axis=1, keepdims=True) + jnp.sum(
        fresh_weights, axis=1, keepdims=True
    )
    numerator = jnp.dot(
        weights.astype(bf16), values, preferred_element_type=f32
    ) + jnp.dot(fresh_weights.astype(bf16), fresh_v, preferred_element_type=f32)
    high = total.astype(bf16).astype(f32)
    lane = lax.broadcasted_iota(jnp.int32, (combos, HD), 1)
    stats = jnp.where(lane < 32, peak, jnp.where(lane < 64, high, total - high))
    stats = jnp.where(lane < 96, stats, gain_row[...][:1])
    out[...] = jnp.concatenate(
        [numerator.reshape(peers, -1, HD), stats.reshape(peers, -1, HD)], axis=1
    ).astype(bf16)


def merge(parts, ordered, out, gain_out):
    x = parts[...].astype(f32)
    count = x.shape[1] // 2
    numerator, stats = x[:, :count], x[:, count:]
    gain_out[...] = jnp.concatenate([stats[:, :1, 96:]] * 4, axis=2)
    peak = stats[:, :, 0:1]
    total = stats[:, :, 32:33] + stats[:, :, 64:65]
    top = jnp.max(peak, axis=0, keepdims=True)
    factor = jnp.exp(peak - top)
    denominator = jnp.sum(factor * total, axis=0)
    value = jnp.sum(factor * numerator, axis=0) / denominator
    value = jnp.broadcast_to(value.astype(bf16)[None], (out.shape[0],) + value.shape)
    out[...] = jnp.concatenate([ordered[...], value], axis=1)


def pack(x):
    return jnp.concatenate([x[8 * q : 8 * q + 8] for q in range(4)], axis=1)


def project(attended, weight, residual, out):
    x = attended[...][:, 16:].astype(f32).reshape(-1, BATCH, HD).astype(bf16)
    flat = jnp.concatenate([x[h] for h in range(x.shape[0])], axis=1)
    acc = jnp.dot(flat, weight[...], preferred_element_type=f32)
    tp = out.shape[0] // 2
    me = lax.axis_index("tp")
    blocks = [
        pack(acc[:, 32 * j : 32 * j + 32]) + jnp.where(me == j, residual[...], 0.0)
        for j in range(tp)
    ]
    out[...] = jnp.stack(blocks * 2, axis=0).astype(bf16)


def add_up(parts, own, sent):
    total = jnp.sum(parts[...].astype(f32).reshape(2, -1, 8, HD), axis=1)
    value = total.reshape(16, HD).astype(bf16)
    wide = value.astype(f32)
    own[...] = jnp.where(lax.axis_index("kvp") % 2 == 0, wide[:8], wide[8:])
    sent[...] = jnp.broadcast_to(value[None], sent.shape)


def feed_forward(
    columns, gain, gate_weight, up_weight, own, pages, out, stream, regrouped, staged, done
):
    wide = own[...]
    staged[...] = jnp.concatenate(
        [wide[:, 32 * q : 32 * q + 32] for q in range(4)], axis=0
    ).astype(bf16)
    copies = [
        pltpu.make_async_copy(pages.at[:, : regrouped.shape[1]], regrouped, done.at[0]),
        pltpu.make_async_copy(staged, stream, done.at[1]),
    ]
    for copy in copies:
        copy.start()
    x = columns[...].astype(f32).reshape(-1, 8, HD)
    square = jnp.sum(x * x, axis=0)
    square = jnp.concatenate(
        [jnp.sum(square[:, 32 * q : 32 * q + 32], axis=1, keepdims=True) for q in range(4)],
        axis=0,
    )
    scaled = (x * gain[...]).reshape(-1, 4, 8, HD)
    lane = lax.broadcasted_iota(jnp.int32, (scaled.shape[0], 8, HD), 2) // 32
    blocks = []
    for q in range(4):
        block = None
        for t in range(4):
            piece = scaled[:, t]
            if t != q:
                piece = pltpu.roll(piece, (t - q) * 32 % HD, 2)
            block = piece if block is None else jnp.where(lane == t, piece, block)
        blocks.append(block)
    rows = jnp.concatenate(blocks, axis=1).astype(bf16)
    flat = jnp.concatenate([rows[g] for g in range(rows.shape[0])], axis=1)
    width = gate_weight.shape[2]
    gate = jnp.dot(flat, gate_weight[...].reshape(-1, width), preferred_element_type=f32)
    up = jnp.dot(flat, up_weight[...].reshape(-1, width), preferred_element_type=f32)
    peers = out.shape[0]
    part = width // peers
    high = square.astype(bf16).astype(f32)
    tail = lax.broadcasted_iota(jnp.int32, (BATCH, 64 - part), 1)
    tail = jnp.where(tail == 0, high, jnp.where(tail == 1, square - high, 0.0))
    gap = jnp.zeros((BATCH, 64 - part), f32)
    for j in range(peers):
        out[j] = jnp.concatenate(
            [
                gate[:, part * j : part * j + part],
                gap,
                up[:, part * j : part * j + part],
                tail,
            ],
            axis=1,
        ).astype(bf16)
    for copy in copies:
        copy.wait()


def activate(parts, out):
    total = jnp.sum(parts[...].astype(f32), axis=0)
    part = out.shape[1]
    square = total[:, 64 + part : 65 + part] + total[:, 65 + part : 66 + part]
    inverse = lax.rsqrt(square / D + epsilon)
    gated = total[:, :part] * inverse
    lifted = total[:, 64 : 64 + part] * inverse
    out[...] = (gated / (1.0 + jnp.exp(-gated)) * lifted).astype(bf16)


def exchange(x, axis, groups=None):
    return lax.all_to_all(
        x, axis, split_axis=0, concat_axis=0, tiled=True, axis_index_groups=groups
    )


def shards(
    queries,
    fresh_kv,
    kv_cache,
    page_owner,
    context_pages,
    residual,
    out_proj,
    norm_gain,
    gate_weight,
    up_weight,
):
    kvp = lax.axis_size("kvp")
    tp = lax.axis_size("tp")
    shape = jax.ShapeDtypeStruct
    combos = queries.shape[2] * BATCH

    count, page_len = kv_cache.shape[0], kv_cache.shape[2]
    tokens = count * page_len
    raw = jnp.concatenate(
        [
            queries.transpose(0, 1, 3, 2),
            fresh_kv[:, :, :, 0].transpose(0, 2, 3, 1),
        ],
        axis=1,
    )
    sent = call(
        pack_inputs,
        "pack_inputs",
        shape((kvp, 2, combos + 4 * BATCH), bf16),
        [VMEM],
        raw,
    )
    gathered = exchange(sent, "kvp")
    keys, values, row_of, ordered, packed, gain_row = call(
        prepare,
        "prepare",
        [
            shape((tokens, HD), bf16),
            shape((tokens, HD), bf16),
            shape((8, tokens), jnp.int32),
            shape((count, 2 * page_len, HD), bf16),
            shape((8, HD), f32),
            shape((8, HD), f32),
        ],
        [SMEM, SMEM, VMEM, VMEM, VMEM],
        context_pages,
        page_owner,
        kv_cache,
        residual,
        norm_gain.reshape(1, -1),
    )
    parts = call(
        attention,
        "attention",
        shape((kvp, 2 * combos // kvp, HD), bf16),
        [VMEM] * 5,
        gathered.reshape(2 * kvp, -1),
        keys,
        values,
        row_of,
        gain_row,
    )
    parts = exchange(parts, "kvp")
    piece, gain_rows = call(
        merge,
        "merge",
        [
            shape((kvp, 2 * page_len + combos // kvp, HD), bf16),
            shape((kvp, 1, HD), f32),
        ],
        [VMEM] * 2,
        parts,
        ordered,
    )
    attended = exchange(piece, "kvp")
    partial = call(
        project,
        "project",
        shape((2 * tp, 8, HD), bf16),
        [VMEM] * 3,
        attended,
        out_proj,
        packed,
    )
    chips = kvp // 2
    chip_line = [[chip * 2 * tp + k for k in range(2 * tp)] for chip in range(chips)]
    same_core = [[2 * chip + core for chip in range(chips)] for core in range(2)]
    summands = exchange(partial, ("kvp", "tp"), chip_line)
    own, block = call(
        add_up,
        "add_up",
        [shape((8, HD), f32), shape((chips, 16, HD), bf16)],
        [VMEM],
        summands,
    )
    columns = exchange(block, "kvp", same_core)
    lifted, stream, regrouped = call(
        feed_forward,
        "feed_forward",
        [
            shape((tp, BATCH, HD), bf16),
            shape(residual.shape, bf16),
            shape((count, 2 * page_len, HD), bf16),
        ],
        [VMEM] * 6,
        columns,
        gain_rows,
        gate_weight,
        up_weight,
        own,
        attended,
        out_specs=[VMEM, HBM, HBM],
        scratch=[pltpu.VMEM(residual.shape, bf16), pltpu.SemaphoreType.DMA((2,))],
    )
    lifted = exchange(lifted, "tp")
    hidden = call(
        activate, "activate", shape((BATCH, gate_weight.shape[2] // tp), bf16), [VMEM], lifted
    )
    return regrouped.reshape(kv_cache.shape), stream, hidden


def solution(mesh):
    return jax.shard_map(
        shards,
        mesh=mesh,
        in_specs=(
            P(None, None, "tp", "kvp"),
            P(None, None, None, "tp", "kvp"),
            P("kvp", None, None, "tp"),
            P(),
            P(),
            P(None, ("kvp", "tp")),
            P("tp", "kvp"),
            P(("kvp", "tp")),
            P(None, "tp", "kvp"),
            P(None, "tp", "kvp"),
        ),
        out_specs=(P("kvp", None, None, "tp"), P(None, ("kvp", "tp")), P(None, ("kvp", "tp"))),
        check_vma=False,
    )
```

```python
import jax
import jax.numpy as jnp
from jax import lax
from jax.experimental import pallas as pl
from jax.experimental.pallas import tpu as pltpu
from jax.sharding import PartitionSpec as P

D = 16384
HEADS = 128
KVH = 8
HD = 128
STEPS = 2
ROWS = 16
BATCH = STEPS * ROWS

negative = -1e30
epsilon = 1e-05
bf16 = jnp.bfloat16
f32 = jnp.float32
VMEM = pl.BlockSpec(memory_space=pltpu.VMEM)
SMEM = pl.BlockSpec(memory_space=pltpu.SMEM)
PARAMS = pltpu.CompilerParams(vmem_limit_bytes=16 * 1024 * 1024)
HBM = pl.BlockSpec(memory_space=pltpu.HBM)


def call(body, name, out_shape, in_specs, *args, out_specs=None, scratch=()):
    if out_specs is None:
        out_specs = [VMEM] * len(out_shape) if isinstance(out_shape, list) else VMEM
    return pl.pallas_call(
        body,
        out_shape=out_shape,
        in_specs=in_specs,
        out_specs=out_specs,
        scratch_shapes=scratch,
        compiler_params=PARAMS,
        name=name,
    )(*args)


def pack_inputs(raw, out):
    heads = raw.shape[3]
    blocks = raw[...].astype(f32)
    rows = blocks[:, :ROWS].reshape(2 * BATCH, heads).astype(bf16)
    entry = lax.broadcasted_iota(jnp.int32, (2 * BATCH, heads * BATCH), 0)
    target = lax.broadcasted_iota(jnp.int32, (2 * BATCH, heads * BATCH), 1)
    head = lax.broadcasted_iota(jnp.int32, (heads, heads * BATCH), 0)
    lane = lax.broadcasted_iota(jnp.int32, (heads, heads * BATCH), 1)
    lines = []
    for d in range(2):
        place = (entry % 2 == d) & (entry // 2 == target % BATCH)
        spread = lax.dot_general(
            rows,
            jnp.where(place, 1.0, 0.0).astype(bf16),
            (((0,), (0,)), ((), ())),
            preferred_element_type=f32,
        )
        lines.append(
            jnp.sum(jnp.where(lane // BATCH == head, spread, 0.0), axis=0, keepdims=True)
        )
    q = jnp.concatenate(lines, axis=0)
    kv = [blocks[u, ROWS + w] for w in range(2) for u in range(STEPS)]
    line = jnp.concatenate([q] + kv + [jnp.zeros((2, 2 * BATCH), f32)], axis=1)
    out[...] = jnp.broadcast_to(line.astype(bf16)[None], out.shape)


def prepare(
    context, owner, pages, residual, gain, keys, values, member, ordered, packed, gain_row
):
    me = lax.axis_index("kvp")
    count, page_len = pages.shape[0], pages.shape[2]
    cache = pages[...].astype(f32)
    keys[...] = cache[:, 0].reshape(-1, HD).astype(bf16)
    values[...] = cache[:, 1].reshape(-1, HD).astype(bf16)
    page = lax.broadcasted_iota(jnp.int32, (8, member.shape[1]), 1) // page_len + me * count
    row = jnp.zeros(page.shape, jnp.int32)
    end = jnp.int32(0)
    for r in range(ROWS - 1):
        end = end + context[r]
        row = row + (page >= end).astype(jnp.int32)
    line = lax.broadcasted_iota(jnp.int32, member.shape, 0) % ROWS
    member[...] = jnp.where(row[:1] == line, 1.0, 0.0)
    packed[...] = pack(residual[...].astype(f32))
    line = gain[...].astype(f32)
    gain_row[...] = jnp.broadcast_to(
        jnp.concatenate([line] * 4, axis=1), gain_row.shape
    )

    def one(c, carry):
        ordered[owner[me * count + c]] = pages[c].reshape(2 * page_len, HD)
        return carry

    lax.fori_loop(0, count, one, 0, unroll=8)


def attention(gathered, key_ref, value_ref, member_ref, gain_row, out):
    turned = gathered[...].astype(f32).reshape(HD, -1).T
    q = turned[: HEADS // KVH * BATCH].astype(bf16)
    fresh = turned[HEADS // KVH * BATCH :].astype(bf16)
    fresh_k, fresh_v = fresh[:BATCH], fresh[BATCH : 2 * BATCH]
    keys, values = key_ref[...], value_ref[...]
    combos, tokens = q.shape[0], keys.shape[0]
    peers = out.shape[0]
    me = lax.axis_index("kvp")
    scale = HD ** (-0.5)
    nt = (((1,), (1,)), ((), ()))
    scores = lax.dot_general(q, keys, nt, preferred_element_type=f32) * scale
    fresh_scores = lax.dot_general(q, fresh_k, nt, preferred_element_type=f32) * scale

    combo = lax.broadcasted_iota(jnp.int32, (combos, 1), 0)
    combo_row = combo % ROWS
    combo_step = (combo // ROWS) % STEPS
    lines = member_ref.shape[0]
    member = jnp.broadcast_to(member_ref[...][None], (combos // lines, lines, tokens))
    member = member.reshape(combos, tokens) > 0.5
    entry = lax.broadcasted_iota(jnp.int32, (1, BATCH), 1)
    fresh_member = (
        (combo_row == entry % ROWS) & (entry // ROWS <= combo_step) & (me == 0)
    )
    scores = jnp.where(member, scores, negative)
    fresh_scores = jnp.where(fresh_member, fresh_scores, negative)
    peak = jnp.maximum(
        jnp.max(scores, axis=1, keepdims=True), jnp.max(fresh_scores, axis=1, keepdims=True)
    )
    peak = peak.astype(bf16).astype(f32)
    weights = jnp.where(member, jnp.exp(scores - peak), 0.0)
    fresh_weights = jnp.where(fresh_member, jnp.exp(fresh_scores - peak), 0.0)
    total = jnp.sum(weights, axis=1, keepdims=True) + jnp.sum(
        fresh_weights, axis=1, keepdims=True
    )
    numerator = jnp.dot(
        weights.astype(bf16), values, preferred_element_type=f32
    ) + jnp.dot(fresh_weights.astype(bf16), fresh_v, preferred_element_type=f32)
    high = total.astype(bf16).astype(f32)
    columns = [x.reshape(peers, 8, 1) for x in (peak, high, total - high)]
    lane = lax.broadcasted_iota(jnp.int32, (peers, 4, HD), 2)
    stats = jnp.broadcast_to(gain_row[...][None, :4], (peers, 4, HD))
    for k in range(5, -1, -1):
        column = columns[k % 3][:, :4] if k < 3 else columns[k % 3][:, 4:]
        stats = jnp.where(lane < 16 * k + 16, column, stats)
    numerator = numerator.reshape(peers, 8, HD)
    out[:, 0] = numerator[:, :4].astype(bf16)
    out[:, 1] = numerator[:, 4:].astype(bf16)
    out[:, 2] = stats.astype(bf16)


def merge(parts, ordered, out, gain_out):
    stats = parts[:, 2].astype(f32)
    gain_out[...] = jnp.concatenate([stats[:, :1, 96:]] * 4, axis=2)
    values = []
    for half in range(2):
        at = 48 * half
        peak = stats[:, :, at : at + 1]
        total = stats[:, :, at + 16 : at + 17] + stats[:, :, at + 32 : at + 33]
        factor = jnp.exp(peak - jnp.max(peak, axis=0, keepdims=True))
        numerator = jnp.sum(factor * parts[:, half].astype(f32), axis=0)
        values.append(numerator / jnp.sum(factor * total, axis=0))
    value = jnp.concatenate(values, axis=0).astype(bf16)
    value = jnp.broadcast_to(value[None], (out.shape[0],) + value.shape)
    out[...] = jnp.concatenate([ordered[...], value], axis=1)


def pack(x):
    return jnp.concatenate([x[8 * q : 8 * q + 8] for q in range(4)], axis=1)


def project(attended, weight, residual, out):
    x = attended[...][:, 16:].astype(f32).reshape(-1, BATCH, HD).astype(bf16)
    flat = jnp.concatenate([x[h] for h in range(x.shape[0])], axis=1)
    acc = jnp.dot(flat, weight[...], preferred_element_type=f32)
    tp = out.shape[0] // 2
    me = lax.axis_index("tp")
    blocks = [
        pack(acc[:, 32 * j : 32 * j + 32]) + jnp.where(me == j, residual[...], 0.0)
        for j in range(tp)
    ]
    out[...] = jnp.stack(blocks * 2, axis=0).astype(bf16)


def add_up(parts, own, sent):
    total = jnp.sum(parts[...].astype(f32).reshape(2, -1, 8, HD), axis=1)
    value = total.reshape(16, HD).astype(bf16)
    wide = value.astype(f32)
    own[...] = jnp.where(lax.axis_index("kvp") % 2 == 0, wide[:8], wide[8:])
    sent[...] = jnp.broadcast_to(value[None], sent.shape)


def feed_forward(
    columns, gain, gate_weight, up_weight, own, pages, out, stream, regrouped, staged, done
):
    wide = own[...]
    staged[...] = jnp.concatenate(
        [wide[:, 32 * q : 32 * q + 32] for q in range(4)], axis=0
    ).astype(bf16)
    copies = [
        pltpu.make_async_copy(pages.at[:, : regrouped.shape[1]], regrouped, done.at[0]),
        pltpu.make_async_copy(staged, stream, done.at[1]),
    ]
    for copy in copies:
        copy.start()
    x = columns[...].astype(f32).reshape(-1, 8, HD)
    square = jnp.sum(x * x, axis=0)
    square = jnp.concatenate(
        [jnp.sum(square[:, 32 * q : 32 * q + 32], axis=1, keepdims=True) for q in range(4)],
        axis=0,
    )
    scaled = (x * gain[...]).reshape(-1, 4, 8, HD)
    lane = lax.broadcasted_iota(jnp.int32, (scaled.shape[0], 8, HD), 2) // 32
    blocks = []
    for q in range(4):
        block = None
        for t in range(4):
            piece = scaled[:, t]
            if t != q:
                piece = pltpu.roll(piece, (t - q) * 32 % HD, 2)
            block = piece if block is None else jnp.where(lane == t, piece, block)
        blocks.append(block)
    rows = jnp.concatenate(blocks, axis=1).astype(bf16)
    flat = jnp.concatenate([rows[g] for g in range(rows.shape[0])], axis=1)
    width = gate_weight.shape[2]
    gate = jnp.dot(flat, gate_weight[...].reshape(-1, width), preferred_element_type=f32)
    up = jnp.dot(flat, up_weight[...].reshape(-1, width), preferred_element_type=f32)
    peers = out.shape[0]
    part = width // peers
    high = square.astype(bf16).astype(f32)
    tail = lax.broadcasted_iota(jnp.int32, (BATCH, 64 - part), 1)
    tail = jnp.where(tail == 0, high, jnp.where(tail == 1, square - high, 0.0))
    gap = jnp.zeros((BATCH, 64 - part), f32)
    for j in range(peers):
        out[j] = jnp.concatenate(
            [
                gate[:, part * j : part * j + part],
                gap,
                up[:, part * j : part * j + part],
                tail,
            ],
            axis=1,
        ).astype(bf16)
    for copy in copies:
        copy.wait()


def activate(parts, out):
    total = jnp.sum(parts[...].astype(f32), axis=0)
    part = out.shape[1]
    square = total[:, 64 + part : 65 + part] + total[:, 65 + part : 66 + part]
    inverse = lax.rsqrt(square / D + epsilon)
    gated = total[:, :part] * inverse
    lifted = total[:, 64 : 64 + part] * inverse
    out[...] = (gated / (1.0 + jnp.exp(-gated)) * lifted).astype(bf16)


def exchange(x, axis, groups=None):
    return lax.all_to_all(
        x, axis, split_axis=0, concat_axis=0, tiled=True, axis_index_groups=groups
    )


def shards(
    queries,
    fresh_kv,
    kv_cache,
    page_owner,
    context_pages,
    residual,
    out_proj,
    norm_gain,
    gate_weight,
    up_weight,
):
    kvp = lax.axis_size("kvp")
    tp = lax.axis_size("tp")
    shape = jax.ShapeDtypeStruct
    combos = queries.shape[2] * BATCH

    count, page_len = kv_cache.shape[0], kv_cache.shape[2]
    tokens = count * page_len
    raw = jnp.concatenate(
        [
            queries.transpose(0, 1, 3, 2),
            fresh_kv[:, :, :, 0].transpose(0, 2, 3, 1),
        ],
        axis=1,
    )
    sent = call(
        pack_inputs,
        "pack_inputs",
        shape((kvp, 2, combos + 4 * BATCH), bf16),
        [VMEM],
        raw,
    )
    gathered = exchange(sent, "kvp")
    keys, values, member, ordered, packed, gain_row = call(
        prepare,
        "prepare",
        [
            shape((tokens, HD), bf16),
            shape((tokens, HD), bf16),
            shape((16 * ROWS, tokens), f32),
            shape((count, 2 * page_len, HD), bf16),
            shape((8, HD), f32),
            shape((8, HD), f32),
        ],
        [SMEM, SMEM, VMEM, VMEM, VMEM],
        context_pages,
        page_owner,
        kv_cache,
        residual,
        norm_gain.reshape(1, -1),
    )
    parts = call(
        attention,
        "attention",
        shape((kvp, 3, 4, HD), bf16),
        [VMEM] * 5,
        gathered,
        keys,
        values,
        member,
        gain_row,
    )
    parts = exchange(parts, "kvp")
    piece, gain_rows = call(
        merge,
        "merge",
        [
            shape((kvp, 2 * page_len + combos // kvp, HD), bf16),
            shape((kvp, 1, HD), f32),
        ],
        [VMEM] * 2,
        parts,
        ordered,
    )
    attended = exchange(piece, "kvp")
    partial = call(
        project,
        "project",
        shape((2 * tp, 8, HD), bf16),
        [VMEM] * 3,
        attended,
        out_proj,
        packed,
    )
    chips = kvp // 2
    chip_line = [[chip * 2 * tp + k for k in range(2 * tp)] for chip in range(chips)]
    same_core = [[2 * chip + core for chip in range(chips)] for core in range(2)]
    summands = exchange(partial, ("kvp", "tp"), chip_line)
    own, block = call(
        add_up,
        "add_up",
        [shape((8, HD), f32), shape((chips, 16, HD), bf16)],
        [VMEM],
        summands,
    )
    columns = exchange(block, "kvp", same_core)
    lifted, stream, regrouped = call(
        feed_forward,
        "feed_forward",
        [
            shape((tp, BATCH, HD), bf16),
            shape(residual.shape, bf16),
            shape((count, 2 * page_len, HD), bf16),
        ],
        [VMEM] * 6,
        columns,
        gain_rows,
        gate_weight,
        up_weight,
        own,
        attended,
        out_specs=[VMEM, HBM, HBM],
        scratch=[pltpu.VMEM(residual.shape, bf16), pltpu.SemaphoreType.DMA((2,))],
    )
    lifted = exchange(lifted, "tp")
    hidden = call(
        activate, "activate", shape((BATCH, gate_weight.shape[2] // tp), bf16), [VMEM], lifted
    )
    return regrouped.reshape(kv_cache.shape), stream, hidden


def solution(mesh):
    return jax.shard_map(
        shards,
        mesh=mesh,
        in_specs=(
            P(None, None, "tp", "kvp"),
            P(None, None, None, "tp", "kvp"),
            P("kvp", None, None, "tp"),
            P(),
            P(),
            P(None, ("kvp", "tp")),
            P("tp", "kvp"),
            P(("kvp", "tp")),
            P(None, "tp", "kvp"),
            P(None, "tp", "kvp"),
        ),
        out_specs=(P("kvp", None, None, "tp"), P(None, ("kvp", "tp")), P(None, ("kvp", "tp"))),
        check_vma=False,
    )
```

```python
import jax
import jax.numpy as jnp
from jax import lax
from jax.experimental import pallas as pl
from jax.experimental.pallas import tpu as pltpu
from jax.sharding import PartitionSpec as P

D = 16384
HEADS = 128
KVH = 8
HD = 128
STEPS = 2
ROWS = 16
BATCH = STEPS * ROWS
LINES = 4 * ROWS

negative = -1e30
epsilon = 1e-05
bf16 = jnp.bfloat16
f32 = jnp.float32
VMEM = pl.BlockSpec(memory_space=pltpu.VMEM)
SMEM = pl.BlockSpec(memory_space=pltpu.SMEM)
PARAMS = pltpu.CompilerParams(vmem_limit_bytes=16 * 1024 * 1024)
HBM = pl.BlockSpec(memory_space=pltpu.HBM)


def call(body, name, out_shape, in_specs, *args, out_specs=None, scratch=()):
    if out_specs is None:
        out_specs = [VMEM] * len(out_shape) if isinstance(out_shape, list) else VMEM
    return pl.pallas_call(
        body,
        out_shape=out_shape,
        in_specs=in_specs,
        out_specs=out_specs,
        scratch_shapes=scratch,
        compiler_params=PARAMS,
        name=name,
    )(*args)


def pack_inputs(raw, out):
    heads = raw.shape[3]
    blocks = raw[...].astype(f32)
    rows = blocks[:, :ROWS].reshape(2 * BATCH, heads).astype(bf16)
    entry = lax.broadcasted_iota(jnp.int32, (2 * BATCH, heads * BATCH), 0)
    target = lax.broadcasted_iota(jnp.int32, (2 * BATCH, heads * BATCH), 1)
    head = lax.broadcasted_iota(jnp.int32, (heads, heads * BATCH), 0)
    lane = lax.broadcasted_iota(jnp.int32, (heads, heads * BATCH), 1)
    lines = []
    for d in range(2):
        place = (entry % 2 == d) & (entry // 2 == target % BATCH)
        spread = lax.dot_general(
            rows,
            jnp.where(place, 1.0, 0.0).astype(bf16),
            (((0,), (0,)), ((), ())),
            preferred_element_type=f32,
        )
        lines.append(
            jnp.sum(jnp.where(lane // BATCH == head, spread, 0.0), axis=0, keepdims=True)
        )
    q = jnp.concatenate(lines, axis=0)
    kv = [blocks[u, ROWS + w] for w in range(2) for u in range(STEPS)]
    tail = kv + [blocks[0, ROWS + 2], blocks[0, ROWS + 3]] * 2
    half = q.shape[1] // 2
    lines = [
        jnp.concatenate([q[:, c * half : c * half + half]] + tail, axis=1).astype(bf16)
        for c in range(2)
    ]
    sent = jnp.stack(lines, axis=0)[None]
    out[...] = jnp.broadcast_to(sent, (out.shape[0] // 2,) + sent.shape[1:]).reshape(out.shape)


def prepare(
    numbers, pages, residual, keys, values, member, ordered, packed
):
    me = lax.axis_index("kvp")
    count, page_len = pages.shape[1], pages.shape[3]
    half = count * page_len
    for c in range(2):
        cache = pages[c].astype(f32)
        keys[c * half : c * half + half] = cache[:, 0].reshape(-1, HD).astype(bf16)
        values[c * half : c * half + half] = cache[:, 1].reshape(-1, HD).astype(bf16)
    page = lax.broadcasted_iota(jnp.int32, (8, member.shape[1]), 1) // page_len
    page = page + me // 2 * 2 * count
    row = jnp.zeros(page.shape, jnp.int32)
    end = jnp.int32(0)
    for r in range(ROWS - 1):
        end = end + numbers[r]
        row = row + (page >= end).astype(jnp.int32)
    line = lax.broadcasted_iota(jnp.int32, member.shape, 0) % ROWS
    member[...] = jnp.where(row[:1] == line, 1.0, 0.0)
    packed[...] = pack(residual[...].astype(f32))

    def one(c, carry):
        ordered[numbers[ROWS + me * count + c]] = pages[me % 2, c].reshape(2 * page_len, HD)
        return carry

    lax.fori_loop(0, count, one, 0, unroll=8)


def attention(gathered, key_ref, value_ref, member_ref, out, gain_out):
    turned = gathered[...].astype(f32).reshape(HD, -1).T
    combos = HEADS // KVH // 2 * BATCH
    q = turned[:combos].astype(bf16)
    fresh = turned[combos:].astype(bf16)
    fresh_k, fresh_v = fresh[:BATCH], fresh[BATCH : 2 * BATCH]
    keys, values = key_ref[...], value_ref[...]
    tokens = keys.shape[0]
    peers = out.shape[0]
    tail = gathered[...].astype(f32).reshape(HD, -1)[:, combos + 2 * BATCH :].astype(bf16)
    take = lax.broadcasted_iota(jnp.int32, (HD // 2, HD), 1) - 2 * lax.broadcasted_iota(
        jnp.int32, (HD // 2, HD), 0
    )
    gain_out[...] = jnp.concatenate(
        [
            jnp.dot(
                jnp.where(take == k, 1.0, 0.0).astype(bf16), tail, preferred_element_type=f32
            )
            for k in range(2)
        ],
        axis=1,
    )
    me = lax.axis_index("kvp")
    scale = HD ** (-0.5)
    nt = (((1,), (1,)), ((), ()))
    scores = lax.dot_general(q, keys, nt, preferred_element_type=f32) * scale
    fresh_scores = lax.dot_general(q, fresh_k, nt, preferred_element_type=f32) * scale

    combo = lax.broadcasted_iota(jnp.int32, (combos, 1), 0)
    combo_row = combo % ROWS
    combo_step = (combo // ROWS) % STEPS
    lines = member_ref.shape[0]
    member = jnp.broadcast_to(member_ref[...][None], (combos // lines, lines, tokens))
    member = member.reshape(combos, tokens) > 0.5
    entry = lax.broadcasted_iota(jnp.int32, (1, BATCH), 1)
    fresh_member = (
        (combo_row == entry % ROWS) & (entry // ROWS <= combo_step) & (me // 2 == 0)
    )
    scores = jnp.where(member, scores, negative)
    fresh_scores = jnp.where(fresh_member, fresh_scores, negative)
    peak = jnp.maximum(
        jnp.max(scores, axis=1, keepdims=True), jnp.max(fresh_scores, axis=1, keepdims=True)
    )
    peak = peak.astype(bf16).astype(f32)
    weights = jnp.where(member, jnp.exp(scores - peak), 0.0)
    fresh_weights = jnp.where(fresh_member, jnp.exp(fresh_scores - peak), 0.0)
    total = jnp.sum(weights, axis=1, keepdims=True) + jnp.sum(
        fresh_weights, axis=1, keepdims=True
    )
    numerator = jnp.dot(
        weights.astype(bf16), values, preferred_element_type=f32
    ) + jnp.dot(fresh_weights.astype(bf16), fresh_v, preferred_element_type=f32)
    high = total.astype(bf16).astype(f32)
    columns = [x.reshape(peers, 8, 1) for x in (peak, high, total - high)]
    lane = lax.broadcasted_iota(jnp.int32, (peers, 4, HD), 2)
    stats = jnp.zeros((peers, 4, HD), f32)
    for k in range(5, -1, -1):
        column = columns[k % 3][:, :4] if k < 3 else columns[k % 3][:, 4:]
        stats = jnp.where(lane < 16 * k + 16, column, stats)
    numerator = numerator.reshape(peers, 8, HD)
    out[:, 0] = numerator[:, :4].astype(bf16)
    out[:, 1] = numerator[:, 4:].astype(bf16)
    out[:, 2] = stats.astype(bf16)


def merge(parts, ordered, out):
    stats = parts[:, 2].astype(f32)
    values = []
    for half in range(2):
        at = 48 * half
        peak = stats[:, :, at : at + 1]
        total = stats[:, :, at + 16 : at + 17] + stats[:, :, at + 32 : at + 33]
        factor = jnp.exp(peak - jnp.max(peak, axis=0, keepdims=True))
        numerator = jnp.sum(factor * parts[:, half].astype(f32), axis=0)
        values.append(numerator / jnp.sum(factor * total, axis=0))
    value = jnp.concatenate(values, axis=0).astype(bf16)
    value = jnp.broadcast_to(value[None], (out.shape[0],) + value.shape)
    out[...] = jnp.concatenate([ordered[...], value], axis=1)


def pack(x):
    return jnp.concatenate([x[8 * q : 8 * q + 8] for q in range(4)], axis=1)


def project(attended, weight, residual, out):
    x = attended[...][:, 16:].astype(f32).reshape(-1, 2, 8, HD)
    x = jnp.concatenate([x[:, c].reshape(-1, BATCH, HD) for c in range(2)], axis=0)
    x = x.astype(bf16)
    flat = jnp.concatenate([x[h] for h in range(x.shape[0])], axis=1)
    acc = jnp.dot(flat, weight[...], preferred_element_type=f32)
    tp = out.shape[0] // 2
    me = lax.axis_index("tp")
    blocks = [
        pack(acc[:, 32 * j : 32 * j + 32]) + jnp.where(me == j, residual[...], 0.0)
        for j in range(tp)
    ]
    out[...] = jnp.stack(blocks * 2, axis=0).astype(bf16)


def add_up(parts, own, sent):
    total = jnp.sum(parts[...].astype(f32).reshape(2, -1, 8, HD), axis=1)
    value = total.reshape(16, HD).astype(bf16)
    wide = value.astype(f32)
    own[...] = jnp.where(lax.axis_index("kvp") % 2 == 0, wide[:8], wide[8:])
    sent[...] = jnp.broadcast_to(value[None], sent.shape)


def feed_forward(
    columns, gain, gate_weight, up_weight, own, pages, out, stream, regrouped, staged, done
):
    wide = own[...]
    staged[...] = jnp.concatenate(
        [wide[:, 32 * q : 32 * q + 32] for q in range(4)], axis=0
    ).astype(bf16)
    copies = [
        pltpu.make_async_copy(pages.at[:, : regrouped.shape[1]], regrouped, done.at[0]),
        pltpu.make_async_copy(staged, stream, done.at[1]),
    ]
    for copy in copies:
        copy.start()
    x = columns[...].astype(f32).reshape(-1, 8, HD)
    square = jnp.sum(x * x, axis=0)
    square = jnp.concatenate(
        [jnp.sum(square[:, 32 * q : 32 * q + 32], axis=1, keepdims=True) for q in range(4)],
        axis=0,
    )
    scaled = (x * gain[...][:, None, :]).reshape(-1, 4, 8, HD)
    lane = lax.broadcasted_iota(jnp.int32, (scaled.shape[0], 8, HD), 2) // 32
    blocks = []
    for q in range(4):
        block = None
        for t in range(4):
            piece = scaled[:, t]
            if t != q:
                piece = pltpu.roll(piece, (t - q) * 32 % HD, 2)
            block = piece if block is None else jnp.where(lane == t, piece, block)
        blocks.append(block)
    rows = jnp.concatenate(blocks, axis=1).astype(bf16)
    flat = jnp.concatenate([rows[g] for g in range(rows.shape[0])], axis=1)
    width = gate_weight.shape[2]
    gate = jnp.dot(flat, gate_weight[...].reshape(-1, width), preferred_element_type=f32)
    up = jnp.dot(flat, up_weight[...].reshape(-1, width), preferred_element_type=f32)
    peers = out.shape[0]
    part = width // peers
    high = square.astype(bf16).astype(f32)
    tail = lax.broadcasted_iota(jnp.int32, (BATCH, 64 - part), 1)
    tail = jnp.where(tail == 0, high, jnp.where(tail == 1, square - high, 0.0))
    gap = jnp.zeros((BATCH, 64 - part), f32)
    for j in range(peers):
        out[j] = jnp.concatenate(
            [
                gate[:, part * j : part * j + part],
                gap,
                up[:, part * j : part * j + part],
                tail,
            ],
            axis=1,
        ).astype(bf16)
    for copy in copies:
        copy.wait()


def activate(parts, out):
    total = jnp.sum(parts[...].astype(f32), axis=0)
    part = out.shape[1]
    square = total[:, 64 + part : 65 + part] + total[:, 65 + part : 66 + part]
    inverse = lax.rsqrt(square / D + epsilon)
    gated = total[:, :part] * inverse
    lifted = total[:, 64 : 64 + part] * inverse
    out[...] = (gated / (1.0 + jnp.exp(-gated)) * lifted).astype(bf16)


def exchange(x, axis, groups=None):
    return lax.all_to_all(
        x, axis, split_axis=0, concat_axis=0, tiled=True, axis_index_groups=groups
    )


def shards(
    queries,
    fresh_kv,
    kv_cache,
    page_owner,
    context_pages,
    residual,
    out_proj,
    norm_gain,
    gate_weight,
    up_weight,
):
    kvp = lax.axis_size("kvp")
    tp = lax.axis_size("tp")
    shape = jax.ShapeDtypeStruct
    combos = queries.shape[2] * BATCH

    count, page_len = kv_cache.shape[0], kv_cache.shape[2]
    tokens = 2 * count * page_len
    raw = jnp.concatenate(
        [
            queries.transpose(0, 1, 3, 2),
            fresh_kv[:, :, :, 0].transpose(0, 2, 3, 1),
            lax.broadcast_in_dim(norm_gain[:ROWS], (STEPS, 1, 2, ROWS), (3,)),
            lax.broadcast_in_dim(norm_gain[ROWS:], (STEPS, 1, 2, ROWS), (3,)),
        ],
        axis=1,
    )
    sent = call(
        pack_inputs,
        "pack_inputs",
        shape((kvp, 2, combos // 2 + 4 * BATCH), bf16),
        [VMEM],
        raw,
    )
    gathered = exchange(sent, "kvp")
    chips = kvp // 2
    chip_line = [[chip * 2 * tp + k for k in range(2 * tp)] for chip in range(chips)]
    same_core = [[2 * chip + core for chip in range(chips)] for core in range(2)]
    same_chip = [[2 * chip, 2 * chip + 1] for chip in range(chips)]
    pages = lax.all_gather(kv_cache, "kvp", axis_index_groups=same_chip)
    keys, values, member, ordered, packed = call(
        prepare,
        "prepare",
        [
            shape((tokens, HD), bf16),
            shape((tokens, HD), bf16),
            shape((LINES, tokens), f32),
            shape((count, 2 * page_len, HD), bf16),
            shape((8, HD), f32),
        ],
        [SMEM, VMEM, VMEM],
        jnp.concatenate([context_pages, page_owner]),
        pages,
        residual,
    )
    parts, gain_rows = call(
        attention,
        "attention",
        [shape((chips, 3, 4, HD), bf16), shape((kvp, HD), f32)],
        [VMEM] * 4,
        gathered,
        keys,
        values,
        member,
    )
    parts = exchange(parts, "kvp", same_core)
    piece = call(
        merge,
        "merge",
        shape((kvp, 2 * page_len + 8, HD), bf16),
        [VMEM] * 2,
        parts,
        ordered,
    )
    attended = exchange(piece, "kvp")
    partial = call(
        project,
        "project",
        shape((2 * tp, 8, HD), bf16),
        [VMEM] * 3,
        attended,
        out_proj,
        packed,
    )
    summands = exchange(partial, ("kvp", "tp"), chip_line)
    own, block = call(
        add_up,
        "add_up",
        [shape((8, HD), f32), shape((chips, 16, HD), bf16)],
        [VMEM],
        summands,
    )
    columns = exchange(block, "kvp", same_core)
    lifted, stream, regrouped = call(
        feed_forward,
        "feed_forward",
        [
            shape((tp, BATCH, HD), bf16),
            shape(residual.shape, bf16),
            shape((count, 2 * page_len, HD), bf16),
        ],
        [VMEM] * 6,
        columns,
        gain_rows,
        gate_weight,
        up_weight,
        own,
        attended,
        out_specs=[VMEM, HBM, HBM],
        scratch=[pltpu.VMEM(residual.shape, bf16), pltpu.SemaphoreType.DMA((2,))],
    )
    lifted = exchange(lifted, "tp")
    hidden = call(
        activate, "activate", shape((BATCH, gate_weight.shape[2] // tp), bf16), [VMEM], lifted
    )
    return regrouped.reshape(kv_cache.shape), stream, hidden


def solution(mesh):
    return jax.shard_map(
        shards,
        mesh=mesh,
        in_specs=(
            P(None, None, "tp", "kvp"),
            P(None, None, None, "tp", "kvp"),
            P("kvp", None, None, "tp"),
            P(),
            P(),
            P(None, ("kvp", "tp")),
            P("tp", "kvp"),
            P(("kvp", "tp")),
            P(None, "tp", "kvp"),
            P(None, "tp", "kvp"),
        ),
        out_specs=(P("kvp", None, None, "tp"), P(None, ("kvp", "tp")), P(None, ("kvp", "tp"))),
        check_vma=False,
    )
```

```python
import jax
import jax.numpy as jnp
from jax import lax
from jax.experimental import pallas as pl
from jax.experimental.pallas import tpu as pltpu
from jax.sharding import PartitionSpec as P

D = 16384
HEADS = 128
KVH = 8
HD = 128
STEPS = 2
ROWS = 16
BATCH = STEPS * ROWS
LINES = 4 * ROWS

negative = -1e30
epsilon = 1e-05
bf16 = jnp.bfloat16
f32 = jnp.float32
VMEM = pl.BlockSpec(memory_space=pltpu.VMEM)
SMEM = pl.BlockSpec(memory_space=pltpu.SMEM)
MIB = 1024 * 1024
ALL = 60 * MIB
HBM = pl.BlockSpec(memory_space=pltpu.HBM)


def call(body, name, out_shape, in_specs, *args, out_specs=None, scratch=(), room=16 * MIB):
    if out_specs is None:
        out_specs = [VMEM] * len(out_shape) if isinstance(out_shape, list) else VMEM
    return pl.pallas_call(
        body,
        out_shape=out_shape,
        in_specs=in_specs,
        out_specs=out_specs,
        scratch_shapes=scratch,
        compiler_params=pltpu.CompilerParams(vmem_limit_bytes=room),
        name=name,
    )(*args)


def pack_inputs(queries_hbm, fresh_hbm, gain_hbm, out, queries, fresh, gain, done):
    copies = [
        pltpu.make_async_copy(source, target, done.at[k])
        for k, (source, target) in enumerate(
            ((queries_hbm, queries), (fresh_hbm, fresh), (gain_hbm, gain))
        )
    ]
    for copy in copies:
        copy.start()
    for copy in copies:
        copy.wait()
    heads = queries.shape[3]
    rows = queries[...].astype(f32).reshape(2 * BATCH, heads).astype(bf16)
    entry = lax.broadcasted_iota(jnp.int32, (2 * BATCH, heads * BATCH), 0)
    target = lax.broadcasted_iota(jnp.int32, (2 * BATCH, heads * BATCH), 1)
    head = lax.broadcasted_iota(jnp.int32, (heads, heads * BATCH), 0)
    lane = lax.broadcasted_iota(jnp.int32, (heads, heads * BATCH), 1)
    lines = []
    for d in range(2):
        place = (entry % 2 == d) & (entry // 2 == target % BATCH)
        spread = lax.dot_general(
            rows,
            jnp.where(place, 1.0, 0.0).astype(bf16),
            (((0,), (0,)), ((), ())),
            preferred_element_type=f32,
        )
        lines.append(
            jnp.sum(jnp.where(lane // BATCH == head, spread, 0.0), axis=0, keepdims=True)
        )
    q = jnp.concatenate(lines, axis=0)
    new = fresh[...].astype(f32)
    kv = [new[u, w] for w in range(2) for u in range(STEPS)]
    g = gain[...].astype(f32)
    g = jnp.concatenate([g, g], axis=1)
    tail = kv + [jnp.concatenate([g, g], axis=0)]
    half = q.shape[1] // 2
    lines = [
        jnp.concatenate([q[:, c * half : c * half + half]] + tail, axis=1).astype(bf16)
        for c in range(2)
    ]
    sent = jnp.stack(lines, axis=0)[None]
    out[...] = jnp.broadcast_to(sent, (out.shape[0] // 2,) + sent.shape[1:]).reshape(out.shape)


def prepare(
    numbers, pages, residual, keys, values, member, ordered, packed
):
    me = lax.axis_index("kvp")
    count, page_len = pages.shape[1], pages.shape[3]
    half = count * page_len
    for c in range(2):
        cache = pages[c].astype(f32)
        keys[c * half : c * half + half] = cache[:, 0].reshape(-1, HD).astype(bf16)
        values[c * half : c * half + half] = cache[:, 1].reshape(-1, HD).astype(bf16)
    page = lax.broadcasted_iota(jnp.int32, (8, member.shape[1]), 1) // page_len
    page = page + me // 2 * 2 * count
    row = jnp.zeros(page.shape, jnp.int32)
    end = jnp.int32(0)
    for r in range(ROWS - 1):
        end = end + numbers[r]
        row = row + (page >= end).astype(jnp.int32)
    line = lax.broadcasted_iota(jnp.int32, member.shape, 0) % ROWS
    member[...] = jnp.where(row[:1] == line, 1.0, 0.0)
    packed[...] = pack(residual[...].astype(f32))

    def one(c, carry):
        ordered[numbers[ROWS + me * count + c]] = pages[me % 2, c].reshape(2 * page_len, HD)
        return carry

    lax.fori_loop(0, count, one, 0, unroll=8)


def attention(gathered, key_ref, value_ref, member_ref, out, gain_out):
    turned = gathered[...].astype(f32).reshape(HD, -1).T
    combos = HEADS // KVH // 2 * BATCH
    q = turned[:combos].astype(bf16)
    fresh = turned[combos:].astype(bf16)
    fresh_k, fresh_v = fresh[:BATCH], fresh[BATCH : 2 * BATCH]
    keys, values = key_ref[...], value_ref[...]
    tokens = keys.shape[0]
    peers = out.shape[0]
    tail = gathered[...].astype(f32).reshape(HD, -1)[:, combos + 2 * BATCH :].astype(bf16)
    take = lax.broadcasted_iota(jnp.int32, (HD // 2, HD), 1) - 2 * lax.broadcasted_iota(
        jnp.int32, (HD // 2, HD), 0
    )
    gain_out[...] = jnp.concatenate(
        [
            jnp.dot(
                jnp.where(take == k, 1.0, 0.0).astype(bf16), tail, preferred_element_type=f32
            )
            for k in range(2)
        ],
        axis=1,
    )
    me = lax.axis_index("kvp")
    scale = HD ** (-0.5)
    nt = (((1,), (1,)), ((), ()))
    scores = lax.dot_general(q, keys, nt, preferred_element_type=f32) * scale
    fresh_scores = lax.dot_general(q, fresh_k, nt, preferred_element_type=f32) * scale

    combo = lax.broadcasted_iota(jnp.int32, (combos, 1), 0)
    combo_row = combo % ROWS
    combo_step = (combo // ROWS) % STEPS
    lines = member_ref.shape[0]
    member = jnp.broadcast_to(member_ref[...][None], (combos // lines, lines, tokens))
    member = member.reshape(combos, tokens) > 0.5
    entry = lax.broadcasted_iota(jnp.int32, (1, BATCH), 1)
    fresh_member = (
        (combo_row == entry % ROWS) & (entry // ROWS <= combo_step) & (me // 2 == 0)
    )
    scores = jnp.where(member, scores, negative)
    fresh_scores = jnp.where(fresh_member, fresh_scores, negative)
    peak = jnp.maximum(
        jnp.max(scores, axis=1, keepdims=True), jnp.max(fresh_scores, axis=1, keepdims=True)
    )
    peak = peak.astype(bf16).astype(f32)
    weights = jnp.where(member, jnp.exp(scores - peak), 0.0)
    fresh_weights = jnp.where(fresh_member, jnp.exp(fresh_scores - peak), 0.0)
    total = jnp.sum(weights, axis=1, keepdims=True) + jnp.sum(
        fresh_weights, axis=1, keepdims=True
    )
    numerator = jnp.dot(
        weights.astype(bf16), values, preferred_element_type=f32
    ) + jnp.dot(fresh_weights.astype(bf16), fresh_v, preferred_element_type=f32)
    high = total.astype(bf16).astype(f32)
    columns = [x.reshape(peers, 8, 1) for x in (peak, high, total - high)]
    lane = lax.broadcasted_iota(jnp.int32, (peers, 4, HD), 2)
    stats = jnp.zeros((peers, 4, HD), f32)
    for k in range(5, -1, -1):
        column = columns[k % 3][:, :4] if k < 3 else columns[k % 3][:, 4:]
        stats = jnp.where(lane < 16 * k + 16, column, stats)
    numerator = numerator.reshape(peers, 8, HD)
    out[:, 0] = numerator[:, :4].astype(bf16)
    out[:, 1] = numerator[:, 4:].astype(bf16)
    out[:, 2] = stats.astype(bf16)


def merge(parts, ordered, out):
    stats = parts[:, 2].astype(f32)
    values = []
    for half in range(2):
        at = 48 * half
        peak = stats[:, :, at : at + 1]
        total = stats[:, :, at + 16 : at + 17] + stats[:, :, at + 32 : at + 33]
        factor = jnp.exp(peak - jnp.max(peak, axis=0, keepdims=True))
        numerator = jnp.sum(factor * parts[:, half].astype(f32), axis=0)
        values.append(numerator / jnp.sum(factor * total, axis=0))
    value = jnp.concatenate(values, axis=0).astype(bf16)
    value = jnp.broadcast_to(value[None], (out.shape[0],) + value.shape)
    out[...] = jnp.concatenate([ordered[...], value], axis=1)


def pack(x):
    return jnp.concatenate([x[8 * q : 8 * q + 8] for q in range(4)], axis=1)


def project(attended, weight, residual, out):
    x = attended[...][:, 16:].astype(f32).reshape(-1, 2, 8, HD)
    x = jnp.concatenate([x[:, c].reshape(-1, BATCH, HD) for c in range(2)], axis=0)
    x = x.astype(bf16)
    flat = jnp.concatenate([x[h] for h in range(x.shape[0])], axis=1)
    acc = jnp.dot(flat, weight[...], preferred_element_type=f32)
    tp = out.shape[0] // 2
    me = lax.axis_index("tp")
    blocks = [
        pack(acc[:, 32 * j : 32 * j + 32]) + jnp.where(me == j, residual[...], 0.0)
        for j in range(tp)
    ]
    out[...] = jnp.stack(blocks * 2, axis=0).astype(bf16)


def add_up(parts, own, sent):
    total = jnp.sum(parts[...].astype(f32).reshape(2, -1, 8, HD), axis=1)
    value = total.reshape(16, HD).astype(bf16)
    wide = value.astype(f32)
    own[...] = jnp.where(lax.axis_index("kvp") % 2 == 0, wide[:8], wide[8:])
    sent[...] = jnp.broadcast_to(value[None], sent.shape)


def feed_forward(
    columns, gain, gate_weight, up_weight, own, pages, out, stream, regrouped, staged, done
):
    wide = own[...]
    staged[...] = jnp.concatenate(
        [wide[:, 32 * q : 32 * q + 32] for q in range(4)], axis=0
    ).astype(bf16)
    copies = [
        pltpu.make_async_copy(pages.at[:, : regrouped.shape[1]], regrouped, done.at[0]),
        pltpu.make_async_copy(staged, stream, done.at[1]),
    ]
    for copy in copies:
        copy.start()
    x = columns[...].astype(f32).reshape(-1, 8, HD)
    square = jnp.sum(x * x, axis=0)
    square = jnp.concatenate(
        [jnp.sum(square[:, 32 * q : 32 * q + 32], axis=1, keepdims=True) for q in range(4)],
        axis=0,
    )
    scaled = (x * gain[...][:, None, :]).reshape(-1, 4, 8, HD)
    lane = lax.broadcasted_iota(jnp.int32, (scaled.shape[0], 8, HD), 2) // 32
    blocks = []
    for q in range(4):
        block = None
        for t in range(4):
            piece = scaled[:, t]
            if t != q:
                piece = pltpu.roll(piece, (t - q) * 32 % HD, 2)
            block = piece if block is None else jnp.where(lane == t, piece, block)
        blocks.append(block)
    rows = jnp.concatenate(blocks, axis=1).astype(bf16)
    flat = jnp.concatenate([rows[g] for g in range(rows.shape[0])], axis=1)
    width = gate_weight.shape[2]
    gate = jnp.dot(flat, gate_weight[...].reshape(-1, width), preferred_element_type=f32)
    up = jnp.dot(flat, up_weight[...].reshape(-1, width), preferred_element_type=f32)
    peers = out.shape[0]
    part = width // peers
    high = square.astype(bf16).astype(f32)
    tail = lax.broadcasted_iota(jnp.int32, (BATCH, 64 - part), 1)
    tail = jnp.where(tail == 0, high, jnp.where(tail == 1, square - high, 0.0))
    gap = jnp.zeros((BATCH, 64 - part), f32)
    for j in range(peers):
        out[j] = jnp.concatenate(
            [
                gate[:, part * j : part * j + part],
                gap,
                up[:, part * j : part * j + part],
                tail,
            ],
            axis=1,
        ).astype(bf16)
    for copy in copies:
        copy.wait()


def activate(parts, out):
    total = jnp.sum(parts[...].astype(f32), axis=0)
    part = out.shape[1]
    square = total[:, 64 + part : 65 + part] + total[:, 65 + part : 66 + part]
    inverse = lax.rsqrt(square / D + epsilon)
    gated = total[:, :part] * inverse
    lifted = total[:, 64 : 64 + part] * inverse
    out[...] = (gated / (1.0 + jnp.exp(-gated)) * lifted).astype(bf16)


def exchange(x, axis, groups=None):
    return lax.all_to_all(
        x, axis, split_axis=0, concat_axis=0, tiled=True, axis_index_groups=groups
    )


def shards(
    queries,
    fresh_kv,
    kv_cache,
    page_owner,
    context_pages,
    residual,
    out_proj,
    norm_gain,
    gate_weight,
    up_weight,
):
    kvp = lax.axis_size("kvp")
    tp = lax.axis_size("tp")
    shape = jax.ShapeDtypeStruct
    combos = queries.shape[2] * BATCH

    count, page_len = kv_cache.shape[0], kv_cache.shape[2]
    tokens = 2 * count * page_len
    raw = (
        queries.transpose(0, 1, 3, 2),
        fresh_kv[:, :, :, 0].transpose(0, 2, 3, 1),
        norm_gain.reshape(1, -1),
    )
    sent = call(
        pack_inputs,
        "pack_inputs",
        shape((kvp, 2, combos // 2 + 4 * BATCH), bf16),
        [HBM] * 3,
        *raw,
        scratch=[pltpu.VMEM(x.shape, bf16) for x in raw] + [pltpu.SemaphoreType.DMA((3,))],
        room=ALL,
    )
    gathered = exchange(sent, "kvp")
    chips = kvp // 2
    chip_line = [[chip * 2 * tp + k for k in range(2 * tp)] for chip in range(chips)]
    same_core = [[2 * chip + core for chip in range(chips)] for core in range(2)]
    same_chip = [[2 * chip, 2 * chip + 1] for chip in range(chips)]
    pages = lax.all_gather(kv_cache, "kvp", axis_index_groups=same_chip)
    keys, values, member, ordered, packed = call(
        prepare,
        "prepare",
        [
            shape((tokens, HD), bf16),
            shape((tokens, HD), bf16),
            shape((LINES, tokens), f32),
            shape((count, 2 * page_len, HD), bf16),
            shape((8, HD), f32),
        ],
        [SMEM, VMEM, VMEM],
        jnp.concatenate([context_pages, page_owner]),
        pages,
        residual,
    )
    parts, gain_rows = call(
        attention,
        "attention",
        [shape((chips, 3, 4, HD), bf16), shape((kvp, HD), f32)],
        [VMEM] * 4,
        gathered,
        keys,
        values,
        member,
    )
    parts = exchange(parts, "kvp", same_core)
    piece = call(
        merge,
        "merge",
        shape((kvp, 2 * page_len + 8, HD), bf16),
        [VMEM] * 2,
        parts,
        ordered,
    )
    attended = exchange(piece, "kvp")
    partial = call(
        project,
        "project",
        shape((2 * tp, 8, HD), bf16),
        [VMEM] * 3,
        attended,
        out_proj,
        packed,
    )
    summands = exchange(partial, ("kvp", "tp"), chip_line)
    own, block = call(
        add_up,
        "add_up",
        [shape((8, HD), f32), shape((chips, 16, HD), bf16)],
        [VMEM],
        summands,
    )
    columns = exchange(block, "kvp", same_core)
    lifted, stream, regrouped = call(
        feed_forward,
        "feed_forward",
        [
            shape((tp, BATCH, HD), bf16),
            shape(residual.shape, bf16),
            shape((count, 2 * page_len, HD), bf16),
        ],
        [VMEM] * 6,
        columns,
        gain_rows,
        gate_weight,
        up_weight,
        own,
        attended,
        out_specs=[VMEM, HBM, HBM],
        scratch=[pltpu.VMEM(residual.shape, bf16), pltpu.SemaphoreType.DMA((2,))],
    )
    lifted = exchange(lifted, "tp")
    hidden = call(
        activate, "activate", shape((BATCH, gate_weight.shape[2] // tp), bf16), [VMEM], lifted
    )
    return regrouped.reshape(kv_cache.shape), stream, hidden


def solution(mesh):
    return jax.shard_map(
        shards,
        mesh=mesh,
        in_specs=(
            P(None, None, "tp", "kvp"),
            P(None, None, None, "tp", "kvp"),
            P("kvp", None, None, "tp"),
            P(),
            P(),
            P(None, ("kvp", "tp")),
            P("tp", "kvp"),
            P(("kvp", "tp")),
            P(None, "tp", "kvp"),
            P(None, "tp", "kvp"),
        ),
        out_specs=(P("kvp", None, None, "tp"), P(None, ("kvp", "tp")), P(None, ("kvp", "tp"))),
        check_vma=False,
    )
```

```python
import jax
import jax.numpy as jnp
from jax import lax
from jax.experimental import pallas as pl
from jax.experimental.pallas import tpu as pltpu
from jax.sharding import PartitionSpec as P

D = 16384
HEADS = 128
KVH = 8
HD = 128
STEPS = 2
ROWS = 16
BATCH = STEPS * ROWS
LINES = 4 * ROWS
UNROLL = 64

negative = -1e30
epsilon = 1e-05
bf16 = jnp.bfloat16
f32 = jnp.float32
VMEM = pl.BlockSpec(memory_space=pltpu.VMEM)
SMEM = pl.BlockSpec(memory_space=pltpu.SMEM)
MIB = 1024 * 1024
ALL = 60 * MIB
HBM = pl.BlockSpec(memory_space=pltpu.HBM)


def call(body, name, out_shape, in_specs, *args, out_specs=None, scratch=(), room=16 * MIB):
    if out_specs is None:
        out_specs = [VMEM] * len(out_shape) if isinstance(out_shape, list) else VMEM
    return pl.pallas_call(
        body,
        out_shape=out_shape,
        in_specs=in_specs,
        out_specs=out_specs,
        scratch_shapes=scratch,
        compiler_params=pltpu.CompilerParams(vmem_limit_bytes=room),
        name=name,
    )(*args)


def pack_inputs(queries_hbm, fresh_hbm, gain_hbm, out, queries, fresh, gain, done):
    copies = [
        pltpu.make_async_copy(source, target, done.at[k])
        for k, (source, target) in enumerate(
            ((queries_hbm, queries), (fresh_hbm, fresh), (gain_hbm, gain))
        )
    ]
    for copy in copies:
        copy.start()
    for copy in copies:
        copy.wait()
    heads = queries.shape[3]
    rows = queries[...].astype(f32).reshape(2 * BATCH, heads).astype(bf16)
    entry = lax.broadcasted_iota(jnp.int32, (2 * BATCH, heads * BATCH), 0)
    target = lax.broadcasted_iota(jnp.int32, (2 * BATCH, heads * BATCH), 1)
    head = lax.broadcasted_iota(jnp.int32, (heads, heads * BATCH), 0)
    lane = lax.broadcasted_iota(jnp.int32, (heads, heads * BATCH), 1)
    lines = []
    for d in range(2):
        place = (entry % 2 == d) & (entry // 2 == target % BATCH)
        spread = lax.dot_general(
            rows,
            jnp.where(place, 1.0, 0.0).astype(bf16),
            (((0,), (0,)), ((), ())),
            preferred_element_type=f32,
        )
        lines.append(
            jnp.sum(jnp.where(lane // BATCH == head, spread, 0.0), axis=0, keepdims=True)
        )
    q = jnp.concatenate(lines, axis=0)
    new = fresh[...].astype(f32)
    kv = [new[u, w] for w in range(2) for u in range(STEPS)]
    g = gain[...].astype(f32)
    g = jnp.concatenate([g, g], axis=1)
    tail = kv + [jnp.concatenate([g, g], axis=0)]
    half = q.shape[1] // 2
    lines = [
        jnp.concatenate([q[:, c * half : c * half + half]] + tail, axis=1).astype(bf16)
        for c in range(2)
    ]
    sent = jnp.stack(lines, axis=0)[None]
    out[...] = jnp.broadcast_to(sent, (out.shape[0] // 2,) + sent.shape[1:]).reshape(out.shape)


def prepare(
    numbers, pages, residual, keys, values, member, ordered, packed
):
    me = lax.axis_index("kvp")
    count, page_len = pages.shape[1], pages.shape[3]
    half = count * page_len
    for c in range(2):
        cache = pages[c].astype(f32)
        keys[c * half : c * half + half] = cache[:, 0].reshape(-1, HD).astype(bf16)
        values[c * half : c * half + half] = cache[:, 1].reshape(-1, HD).astype(bf16)
    page = lax.broadcasted_iota(jnp.int32, (8, member.shape[1]), 1) // page_len
    page = page + me // 2 * 2 * count
    row = jnp.zeros(page.shape, jnp.int32)
    end = jnp.int32(0)
    for r in range(ROWS - 1):
        end = end + numbers[r]
        row = row + (page >= end).astype(jnp.int32)
    line = lax.broadcasted_iota(jnp.int32, member.shape, 0) % ROWS
    member[...] = jnp.where(row[:1] == line, 1.0, 0.0)
    packed[...] = pack(residual[...].astype(f32))

    first = ROWS + me // 2 * 2 * count

    def one(c, carry):
        for core in range(2):
            place = numbers[first + core * count + c]
            ordered[place, core * 2 * page_len : (core + 1) * 2 * page_len] = pages[
                core, c
            ].reshape(2 * page_len, HD)
        return carry

    lax.fori_loop(0, count, one, 0, unroll=UNROLL)


def attention(gathered, key_ref, value_ref, member_ref, out, gain_out):
    turned = gathered[...].astype(f32).reshape(HD, -1).T
    combos = HEADS // KVH // 2 * BATCH
    q = turned[:combos].astype(bf16)
    fresh = turned[combos:].astype(bf16)
    fresh_k, fresh_v = fresh[:BATCH], fresh[BATCH : 2 * BATCH]
    keys, values = key_ref[...], value_ref[...]
    tokens = keys.shape[0]
    peers = out.shape[0]
    tail = gathered[...].astype(f32).reshape(HD, -1)[:, combos + 2 * BATCH :].astype(bf16)
    take = lax.broadcasted_iota(jnp.int32, (HD // 2, HD), 1) - 2 * lax.broadcasted_iota(
        jnp.int32, (HD // 2, HD), 0
    )
    gain_out[...] = jnp.concatenate(
        [
            jnp.dot(
                jnp.where(take == k, 1.0, 0.0).astype(bf16), tail, preferred_element_type=f32
            )
            for k in range(2)
        ],
        axis=1,
    )
    me = lax.axis_index("kvp")
    scale = HD ** (-0.5)
    nt = (((1,), (1,)), ((), ()))
    scores = lax.dot_general(q, keys, nt, preferred_element_type=f32) * scale
    fresh_scores = lax.dot_general(q, fresh_k, nt, preferred_element_type=f32) * scale

    combo = lax.broadcasted_iota(jnp.int32, (combos, 1), 0)
    combo_row = combo % ROWS
    combo_step = (combo // ROWS) % STEPS
    lines = member_ref.shape[0]
    member = jnp.broadcast_to(member_ref[...][None], (combos // lines, lines, tokens))
    member = member.reshape(combos, tokens) > 0.5
    entry = lax.broadcasted_iota(jnp.int32, (1, BATCH), 1)
    fresh_member = (
        (combo_row == entry % ROWS) & (entry // ROWS <= combo_step) & (me // 2 == 0)
    )
    scores = jnp.where(member, scores, negative)
    fresh_scores = jnp.where(fresh_member, fresh_scores, negative)
    peak = jnp.maximum(
        jnp.max(scores, axis=1, keepdims=True), jnp.max(fresh_scores, axis=1, keepdims=True)
    )
    peak = peak.astype(bf16).astype(f32)
    weights = jnp.where(member, jnp.exp(scores - peak), 0.0)
    fresh_weights = jnp.where(fresh_member, jnp.exp(fresh_scores - peak), 0.0)
    total = jnp.sum(weights, axis=1, keepdims=True) + jnp.sum(
        fresh_weights, axis=1, keepdims=True
    )
    numerator = jnp.dot(
        weights.astype(bf16), values, preferred_element_type=f32
    ) + jnp.dot(fresh_weights.astype(bf16), fresh_v, preferred_element_type=f32)
    high = total.astype(bf16).astype(f32)
    columns = [x.reshape(peers, 8, 1) for x in (peak, high, total - high)]
    lane = lax.broadcasted_iota(jnp.int32, (peers, 4, HD), 2)
    stats = jnp.zeros((peers, 4, HD), f32)
    for k in range(5, -1, -1):
        column = columns[k % 3][:, :4] if k < 3 else columns[k % 3][:, 4:]
        stats = jnp.where(lane < 16 * k + 16, column, stats)
    numerator = numerator.reshape(peers, 8, HD)
    out[:, 0] = numerator[:, :4].astype(bf16)
    out[:, 1] = numerator[:, 4:].astype(bf16)
    out[:, 2] = stats.astype(bf16)


def merge(parts, ordered, out):
    stats = parts[:, 2].astype(f32)
    values = []
    for half in range(2):
        at = 48 * half
        peak = stats[:, :, at : at + 1]
        total = stats[:, :, at + 16 : at + 17] + stats[:, :, at + 32 : at + 33]
        factor = jnp.exp(peak - jnp.max(peak, axis=0, keepdims=True))
        numerator = jnp.sum(factor * parts[:, half].astype(f32), axis=0)
        values.append(numerator / jnp.sum(factor * total, axis=0))
    value = jnp.concatenate(values, axis=0).astype(bf16)
    value = jnp.broadcast_to(value[None], (out.shape[0],) + value.shape)
    out[...] = jnp.concatenate([ordered[: out.shape[0]], value], axis=1)


def pack(x):
    return jnp.concatenate([x[8 * q : 8 * q + 8] for q in range(4)], axis=1)


def project(attended, weight, residual, out):
    x = attended[...].astype(f32).reshape(-1, BATCH, HD).astype(bf16)
    flat = jnp.concatenate([x[h] for h in range(x.shape[0])], axis=1)
    acc = jnp.dot(flat, weight[...], preferred_element_type=f32)
    tp = out.shape[0] // 2
    me = lax.axis_index("tp")
    blocks = [
        pack(acc[:, 32 * j : 32 * j + 32]) + jnp.where(me == j, residual[...], 0.0)
        for j in range(tp)
    ]
    out[...] = jnp.stack(blocks * 2, axis=0).astype(bf16)


def add_up(parts, own, sent):
    total = jnp.sum(parts[...].astype(f32).reshape(2, -1, 8, HD), axis=1)
    value = total.reshape(16, HD).astype(bf16)
    wide = value.astype(f32)
    own[...] = jnp.where(lax.axis_index("kvp") % 2 == 0, wide[:8], wide[8:])
    sent[...] = jnp.broadcast_to(value[None], sent.shape)


def feed_forward(
    columns, gain, gate_weight, up_weight, own, pages, out, stream, regrouped, staged, done
):
    wide = own[...]
    staged[...] = jnp.concatenate(
        [wide[:, 32 * q : 32 * q + 32] for q in range(4)], axis=0
    ).astype(bf16)
    copies = [
        pltpu.make_async_copy(pages.at[:, : regrouped.shape[1]], regrouped, done.at[0]),
        pltpu.make_async_copy(staged, stream, done.at[1]),
    ]
    for copy in copies:
        copy.start()
    x = columns[...].astype(f32).reshape(-1, 8, HD)
    square = jnp.sum(x * x, axis=0)
    square = jnp.concatenate(
        [jnp.sum(square[:, 32 * q : 32 * q + 32], axis=1, keepdims=True) for q in range(4)],
        axis=0,
    )
    scaled = (x * gain[...][:, None, :]).reshape(-1, 4, 8, HD)
    lane = lax.broadcasted_iota(jnp.int32, (scaled.shape[0], 8, HD), 2) // 32
    blocks = []
    for q in range(4):
        block = None
        for t in range(4):
            piece = scaled[:, t]
            if t != q:
                piece = pltpu.roll(piece, (t - q) * 32 % HD, 2)
            block = piece if block is None else jnp.where(lane == t, piece, block)
        blocks.append(block)
    rows = jnp.concatenate(blocks, axis=1).astype(bf16)
    flat = jnp.concatenate([rows[g] for g in range(rows.shape[0])], axis=1)
    width = gate_weight.shape[2]
    gate = jnp.dot(flat, gate_weight[...].reshape(-1, width), preferred_element_type=f32)
    up = jnp.dot(flat, up_weight[...].reshape(-1, width), preferred_element_type=f32)
    peers = out.shape[0]
    part = width // peers
    high = square.astype(bf16).astype(f32)
    tail = lax.broadcasted_iota(jnp.int32, (BATCH, 64 - part), 1)
    tail = jnp.where(tail == 0, high, jnp.where(tail == 1, square - high, 0.0))
    gap = jnp.zeros((BATCH, 64 - part), f32)
    for j in range(peers):
        out[j] = jnp.concatenate(
            [
                gate[:, part * j : part * j + part],
                gap,
                up[:, part * j : part * j + part],
                tail,
            ],
            axis=1,
        ).astype(bf16)
    for copy in copies:
        copy.wait()


def activate(parts, out):
    total = jnp.sum(parts[...].astype(f32), axis=0)
    part = out.shape[1]
    square = total[:, 64 + part : 65 + part] + total[:, 65 + part : 66 + part]
    inverse = lax.rsqrt(square / D + epsilon)
    gated = total[:, :part] * inverse
    lifted = total[:, 64 : 64 + part] * inverse
    out[...] = (gated / (1.0 + jnp.exp(-gated)) * lifted).astype(bf16)


def exchange(x, axis, groups=None):
    return lax.all_to_all(
        x, axis, split_axis=0, concat_axis=0, tiled=True, axis_index_groups=groups
    )


def shards(
    queries,
    fresh_kv,
    kv_cache,
    page_owner,
    context_pages,
    residual,
    out_proj,
    norm_gain,
    gate_weight,
    up_weight,
):
    kvp = lax.axis_size("kvp")
    tp = lax.axis_size("tp")
    shape = jax.ShapeDtypeStruct
    combos = queries.shape[2] * BATCH

    count, page_len = kv_cache.shape[0], kv_cache.shape[2]
    tokens = 2 * count * page_len
    raw = (
        queries.transpose(0, 1, 3, 2),
        fresh_kv[:, :, :, 0].transpose(0, 2, 3, 1),
        norm_gain.reshape(1, -1),
    )
    sent = call(
        pack_inputs,
        "pack_inputs",
        shape((kvp, 2, combos // 2 + 4 * BATCH), bf16),
        [HBM] * 3,
        *raw,
        scratch=[pltpu.VMEM(x.shape, bf16) for x in raw] + [pltpu.SemaphoreType.DMA((3,))],
        room=ALL,
    )
    gathered = exchange(sent, "kvp")
    chips = kvp // 2
    chip_line = [[chip * 2 * tp + k for k in range(2 * tp)] for chip in range(chips)]
    same_core = [[2 * chip + core for chip in range(chips)] for core in range(2)]
    same_chip = [[2 * chip, 2 * chip + 1] for chip in range(chips)]
    numbers = jnp.concatenate([context_pages, page_owner])
    mine = (numbers ^ lax.axis_index("kvp")) & 1 == 0
    place = jnp.where(mine, numbers >> 1, chips)
    index = lax.iota(jnp.int32, numbers.shape[0])
    numbers = jnp.where(index < ROWS, numbers, place)
    pages = lax.all_gather(kv_cache, "kvp", axis_index_groups=same_chip)
    keys, values, member, ordered, packed = call(
        prepare,
        "prepare",
        [
            shape((tokens, HD), bf16),
            shape((tokens, HD), bf16),
            shape((LINES, tokens), f32),
            shape((chips + 1, 4 * page_len, HD), bf16),
            shape((8, HD), f32),
        ],
        [SMEM, VMEM, VMEM],
        numbers,
        pages,
        residual,
    )
    parts, gain_rows = call(
        attention,
        "attention",
        [shape((chips, 3, 4, HD), bf16), shape((kvp, HD), f32)],
        [VMEM] * 4,
        gathered,
        keys,
        values,
        member,
    )
    parts = exchange(parts, "kvp", same_core)
    piece = call(
        merge,
        "merge",
        shape((chips, 4 * page_len + 8, HD), bf16),
        [VMEM] * 2,
        parts,
        ordered,
    )
    arrived = exchange(piece, "kvp", same_core)
    attended = lax.all_gather(
        arrived[:, 4 * page_len :], "kvp", axis_index_groups=same_chip
    )
    partial = call(
        project,
        "project",
        shape((2 * tp, 8, HD), bf16),
        [VMEM] * 3,
        attended,
        out_proj,
        packed,
    )
    summands = exchange(partial, ("kvp", "tp"), chip_line)
    own, block = call(
        add_up,
        "add_up",
        [shape((8, HD), f32), shape((chips, 16, HD), bf16)],
        [VMEM],
        summands,
    )
    columns = exchange(block, "kvp", same_core)
    lifted, stream, regrouped = call(
        feed_forward,
        "feed_forward",
        [
            shape((tp, BATCH, HD), bf16),
            shape(residual.shape, bf16),
            shape((chips, 4 * page_len, HD), bf16),
        ],
        [VMEM] * 6,
        columns,
        gain_rows,
        gate_weight,
        up_weight,
        own,
        arrived,
        out_specs=[VMEM, HBM, HBM],
        scratch=[pltpu.VMEM(residual.shape, bf16), pltpu.SemaphoreType.DMA((2,))],
    )
    lifted = exchange(lifted, "tp")
    hidden = call(
        activate, "activate", shape((BATCH, gate_weight.shape[2] // tp), bf16), [VMEM], lifted
    )
    return regrouped.reshape(kv_cache.shape), stream, hidden


def solution(mesh):
    return jax.shard_map(
        shards,
        mesh=mesh,
        in_specs=(
            P(None, None, "tp", "kvp"),
            P(None, None, None, "tp", "kvp"),
            P("kvp", None, None, "tp"),
            P(),
            P(),
            P(None, ("kvp", "tp")),
            P("tp", "kvp"),
            P(("kvp", "tp")),
            P(None, "tp", "kvp"),
            P(None, "tp", "kvp"),
        ),
        out_specs=(P("kvp", None, None, "tp"), P(None, ("kvp", "tp")), P(None, ("kvp", "tp"))),
        check_vma=False,
    )
```

```python
import jax
import jax.numpy as jnp
from jax import lax
from jax.experimental import pallas as pl
from jax.experimental.pallas import tpu as pltpu
from jax.sharding import PartitionSpec as P

D = 16384
HEADS = 128
KVH = 8
HD = 128
STEPS = 2
ROWS = 16
BATCH = STEPS * ROWS
LINES = 4 * ROWS
UNROLL = 64

negative = -1e30
epsilon = 1e-05
bf16 = jnp.bfloat16
f32 = jnp.float32
VMEM = pl.BlockSpec(memory_space=pltpu.VMEM)
SMEM = pl.BlockSpec(memory_space=pltpu.SMEM)
MIB = 1024 * 1024
ALL = 60 * MIB
HBM = pl.BlockSpec(memory_space=pltpu.HBM)


def call(body, name, out_shape, in_specs, *args, out_specs=None, scratch=(), room=16 * MIB):
    if out_specs is None:
        out_specs = [VMEM] * len(out_shape) if isinstance(out_shape, list) else VMEM
    return pl.pallas_call(
        body,
        out_shape=out_shape,
        in_specs=in_specs,
        out_specs=out_specs,
        scratch_shapes=scratch,
        compiler_params=pltpu.CompilerParams(vmem_limit_bytes=room),
        name=name,
    )(*args)


def pack_inputs(*refs):
    sources, (out, table), targets, done = refs[:6], refs[6:8], refs[8:14], refs[14]
    queries, fresh, gain, residual, owner, context = targets
    copies = [
        pltpu.make_async_copy(source, target, done.at[k])
        for k, (source, target) in enumerate(zip(sources, targets))
    ]
    for copy in copies:
        copy.start()
    for copy in copies:
        copy.wait()
    heads = queries.shape[3]
    rows = queries[...].astype(f32).reshape(2 * BATCH, heads).astype(bf16)
    entry = lax.broadcasted_iota(jnp.int32, (2 * BATCH, heads * BATCH), 0)
    target = lax.broadcasted_iota(jnp.int32, (2 * BATCH, heads * BATCH), 1)
    head = lax.broadcasted_iota(jnp.int32, (heads, heads * BATCH), 0)
    lane = lax.broadcasted_iota(jnp.int32, (heads, heads * BATCH), 1)
    lines = []
    for d in range(2):
        place = (entry % 2 == d) & (entry // 2 == target % BATCH)
        spread = lax.dot_general(
            rows,
            jnp.where(place, 1.0, 0.0).astype(bf16),
            (((0,), (0,)), ((), ())),
            preferred_element_type=f32,
        )
        lines.append(
            jnp.sum(jnp.where(lane // BATCH == head, spread, 0.0), axis=0, keepdims=True)
        )
    q = jnp.concatenate(lines, axis=0)
    new = fresh[...].astype(f32)
    kv = [new[u, w] for w in range(2) for u in range(STEPS)]
    g = gain[...].astype(f32)
    g = jnp.concatenate([g, g], axis=1)
    tail = kv + [jnp.concatenate([g, g], axis=0)]
    half = q.shape[1] // 2
    lines = [
        jnp.concatenate([q[:, c * half : c * half + half]] + tail, axis=1).astype(bf16)
        for c in range(2)
    ]
    sent = jnp.stack(lines, axis=0)[None]
    out[...] = jnp.broadcast_to(sent, (out.shape[0] // 2,) + sent.shape[1:]).reshape(out.shape)
    me = lax.axis_index("kvp")
    line = lax.broadcasted_iota(jnp.int32, owner.shape, 0)
    to = jnp.sum(jnp.where(line == me // 2, owner[...], 0), axis=0, keepdims=True)
    place = jnp.where((to ^ me) & 1 == 0, to >> 1, owner.shape[0])
    spans = jnp.concatenate(
        [context[...], jnp.zeros((1, HD - context.shape[1]), jnp.int32)], axis=1
    )
    table[...] = jnp.concatenate(
        [
            pack(residual[...].astype(f32)),
            place.astype(f32),
            spans.astype(f32),
            jnp.zeros((6, HD), f32),
        ],
        axis=0,
    )


def prepare(
    numbers, table, pages, keys, values, member, ordered, packed
):
    me = lax.axis_index("kvp")
    count, page_len = pages.shape[1], pages.shape[3]
    half = count * page_len
    for c in range(2):
        cache = pages[c].astype(f32)
        keys[c * half : c * half + half] = cache[:, 0].reshape(-1, HD).astype(bf16)
        values[c * half : c * half + half] = cache[:, 1].reshape(-1, HD).astype(bf16)
    page = lax.broadcasted_iota(jnp.int32, (8, member.shape[1]), 1) // page_len
    page = page + me // 2 * 2 * count
    row = jnp.zeros(page.shape, jnp.int32)
    end = jnp.int32(0)
    for r in range(ROWS - 1):
        end = end + numbers[9, r].astype(jnp.int32)
        row = row + (page >= end).astype(jnp.int32)
    line = lax.broadcasted_iota(jnp.int32, member.shape, 0) % ROWS
    member[...] = jnp.where(row[:1] == line, 1.0, 0.0)
    packed[...] = table[:8]


    def one(c, carry):
        for core in range(2):
            place = numbers[8, core * count + c].astype(jnp.int32)
            ordered[place, core * 2 * page_len : (core + 1) * 2 * page_len] = pages[
                core, c
            ].reshape(2 * page_len, HD)
        return carry

    lax.fori_loop(0, count, one, 0, unroll=UNROLL)


def attention(gathered, key_ref, value_ref, member_ref, out, gain_out):
    turned = gathered[...].astype(f32).reshape(HD, -1).T
    combos = HEADS // KVH // 2 * BATCH
    q = turned[:combos].astype(bf16)
    fresh = turned[combos:].astype(bf16)
    fresh_k, fresh_v = fresh[:BATCH], fresh[BATCH : 2 * BATCH]
    keys, values = key_ref[...], value_ref[...]
    tokens = keys.shape[0]
    peers = out.shape[0]
    tail = gathered[...].astype(f32).reshape(HD, -1)[:, combos + 2 * BATCH :].astype(bf16)
    take = lax.broadcasted_iota(jnp.int32, (HD // 2, HD), 1) - 2 * lax.broadcasted_iota(
        jnp.int32, (HD // 2, HD), 0
    )
    gain_out[...] = jnp.concatenate(
        [
            jnp.dot(
                jnp.where(take == k, 1.0, 0.0).astype(bf16), tail, preferred_element_type=f32
            )
            for k in range(2)
        ],
        axis=1,
    )
    me = lax.axis_index("kvp")
    scale = HD ** (-0.5)
    nt = (((1,), (1,)), ((), ()))
    scores = lax.dot_general(q, keys, nt, preferred_element_type=f32) * scale
    fresh_scores = lax.dot_general(q, fresh_k, nt, preferred_element_type=f32) * scale

    combo = lax.broadcasted_iota(jnp.int32, (combos, 1), 0)
    combo_row = combo % ROWS
    combo_step = (combo // ROWS) % STEPS
    lines = member_ref.shape[0]
    member = jnp.broadcast_to(member_ref[...][None], (combos // lines, lines, tokens))
    member = member.reshape(combos, tokens) > 0.5
    entry = lax.broadcasted_iota(jnp.int32, (1, BATCH), 1)
    fresh_member = (
        (combo_row == entry % ROWS) & (entry // ROWS <= combo_step) & (me // 2 == 0)
    )
    scores = jnp.where(member, scores, negative)
    fresh_scores = jnp.where(fresh_member, fresh_scores, negative)
    peak = jnp.maximum(
        jnp.max(scores, axis=1, keepdims=True), jnp.max(fresh_scores, axis=1, keepdims=True)
    )
    peak = peak.astype(bf16).astype(f32)
    weights = jnp.where(member, jnp.exp(scores - peak), 0.0)
    fresh_weights = jnp.where(fresh_member, jnp.exp(fresh_scores - peak), 0.0)
    total = jnp.sum(weights, axis=1, keepdims=True) + jnp.sum(
        fresh_weights, axis=1, keepdims=True
    )
    numerator = jnp.dot(
        weights.astype(bf16), values, preferred_element_type=f32
    ) + jnp.dot(fresh_weights.astype(bf16), fresh_v, preferred_element_type=f32)
    high = total.astype(bf16).astype(f32)
    columns = [x.reshape(peers, 8, 1) for x in (peak, high, total - high)]
    lane = lax.broadcasted_iota(jnp.int32, (peers, 4, HD), 2)
    stats = jnp.zeros((peers, 4, HD), f32)
    for k in range(5, -1, -1):
        column = columns[k % 3][:, :4] if k < 3 else columns[k % 3][:, 4:]
        stats = jnp.where(lane < 16 * k + 16, column, stats)
    numerator = numerator.reshape(peers, 8, HD)
    out[:, 0] = numerator[:, :4].astype(bf16)
    out[:, 1] = numerator[:, 4:].astype(bf16)
    out[:, 2] = stats.astype(bf16)


def merge(parts, ordered, out):
    stats = parts[:, 2].astype(f32)
    values = []
    for half in range(2):
        at = 48 * half
        peak = stats[:, :, at : at + 1]
        total = stats[:, :, at + 16 : at + 17] + stats[:, :, at + 32 : at + 33]
        factor = jnp.exp(peak - jnp.max(peak, axis=0, keepdims=True))
        numerator = jnp.sum(factor * parts[:, half].astype(f32), axis=0)
        values.append(numerator / jnp.sum(factor * total, axis=0))
    value = jnp.concatenate(values, axis=0).astype(bf16)
    value = jnp.broadcast_to(value[None], (out.shape[0],) + value.shape)
    out[...] = jnp.concatenate([ordered[: out.shape[0]], value], axis=1)


def pack(x):
    return jnp.concatenate([x[8 * q : 8 * q + 8] for q in range(4)], axis=1)


def project(attended, weight, residual, out):
    x = attended[...].astype(f32).reshape(-1, BATCH, HD).astype(bf16)
    flat = jnp.concatenate([x[h] for h in range(x.shape[0])], axis=1)
    acc = jnp.dot(flat, weight[...], preferred_element_type=f32)
    tp = out.shape[0] // 2
    me = lax.axis_index("tp")
    blocks = [
        pack(acc[:, 32 * j : 32 * j + 32]) + jnp.where(me == j, residual[...], 0.0)
        for j in range(tp)
    ]
    out[...] = jnp.stack(blocks * 2, axis=0).astype(bf16)


def add_up(parts, own, sent):
    total = jnp.sum(parts[...].astype(f32).reshape(2, -1, 8, HD), axis=1)
    value = total.reshape(16, HD).astype(bf16)
    wide = value.astype(f32)
    own[...] = jnp.where(lax.axis_index("kvp") % 2 == 0, wide[:8], wide[8:])
    sent[...] = jnp.broadcast_to(value[None], sent.shape)


def feed_forward(
    columns, gain, gate_weight, up_weight, own, pages, out, stream, regrouped, staged, done
):
    wide = own[...]
    staged[...] = jnp.concatenate(
        [wide[:, 32 * q : 32 * q + 32] for q in range(4)], axis=0
    ).astype(bf16)
    copies = [
        pltpu.make_async_copy(pages.at[:, : regrouped.shape[1]], regrouped, done.at[0]),
        pltpu.make_async_copy(staged, stream, done.at[1]),
    ]
    for copy in copies:
        copy.start()
    x = columns[...].astype(f32).reshape(-1, 8, HD)
    square = jnp.sum(x * x, axis=0)
    square = jnp.concatenate(
        [jnp.sum(square[:, 32 * q : 32 * q + 32], axis=1, keepdims=True) for q in range(4)],
        axis=0,
    )
    scaled = (x * gain[...][:, None, :]).reshape(-1, 4, 8, HD)
    lane = lax.broadcasted_iota(jnp.int32, (scaled.shape[0], 8, HD), 2) // 32
    blocks = []
    for q in range(4):
        block = None
        for t in range(4):
            piece = scaled[:, t]
            if t != q:
                piece = pltpu.roll(piece, (t - q) * 32 % HD, 2)
            block = piece if block is None else jnp.where(lane == t, piece, block)
        blocks.append(block)
    rows = jnp.concatenate(blocks, axis=1).astype(bf16)
    flat = jnp.concatenate([rows[g] for g in range(rows.shape[0])], axis=1)
    width = gate_weight.shape[2]
    gate = jnp.dot(flat, gate_weight[...].reshape(-1, width), preferred_element_type=f32)
    up = jnp.dot(flat, up_weight[...].reshape(-1, width), preferred_element_type=f32)
    peers = out.shape[0]
    part = width // peers
    high = square.astype(bf16).astype(f32)
    tail = lax.broadcasted_iota(jnp.int32, (BATCH, 64 - part), 1)
    tail = jnp.where(tail == 0, high, jnp.where(tail == 1, square - high, 0.0))
    gap = jnp.zeros((BATCH, 64 - part), f32)
    for j in range(peers):
        out[j] = jnp.concatenate(
            [
                gate[:, part * j : part * j + part],
                gap,
                up[:, part * j : part * j + part],
                tail,
            ],
            axis=1,
        ).astype(bf16)
    for copy in copies:
        copy.wait()


def activate(parts, out):
    total = jnp.sum(parts[...].astype(f32), axis=0)
    part = out.shape[1]
    square = total[:, 64 + part : 65 + part] + total[:, 65 + part : 66 + part]
    inverse = lax.rsqrt(square / D + epsilon)
    gated = total[:, :part] * inverse
    lifted = total[:, 64 : 64 + part] * inverse
    out[...] = (gated / (1.0 + jnp.exp(-gated)) * lifted).astype(bf16)


def exchange(x, axis, groups=None):
    return lax.all_to_all(
        x, axis, split_axis=0, concat_axis=0, tiled=True, axis_index_groups=groups
    )


def shards(
    queries,
    fresh_kv,
    kv_cache,
    page_owner,
    context_pages,
    residual,
    out_proj,
    norm_gain,
    gate_weight,
    up_weight,
):
    kvp = lax.axis_size("kvp")
    tp = lax.axis_size("tp")
    shape = jax.ShapeDtypeStruct
    combos = queries.shape[2] * BATCH

    count, page_len = kv_cache.shape[0], kv_cache.shape[2]
    tokens = 2 * count * page_len
    raw = (
        queries.transpose(0, 1, 3, 2),
        fresh_kv[:, :, :, 0].transpose(0, 2, 3, 1),
        norm_gain.reshape(1, -1),
        residual,
        page_owner.reshape(-1, HD),
        context_pages.reshape(1, -1),
    )
    sent, table = call(
        pack_inputs,
        "pack_inputs",
        [shape((kvp, 2, combos // 2 + 4 * BATCH), bf16), shape((16, HD), f32)],
        [HBM] * 6,
        *raw,
        scratch=[pltpu.VMEM(x.shape, x.dtype) for x in raw] + [pltpu.SemaphoreType.DMA((6,))],
        room=ALL,
    )
    gathered = exchange(sent, "kvp")
    chips = kvp // 2
    chip_line = [[chip * 2 * tp + k for k in range(2 * tp)] for chip in range(chips)]
    same_core = [[2 * chip + core for chip in range(chips)] for core in range(2)]
    same_chip = [[2 * chip, 2 * chip + 1] for chip in range(chips)]
    pages = lax.all_gather(kv_cache, "kvp", axis_index_groups=same_chip)
    keys, values, member, ordered, packed = call(
        prepare,
        "prepare",
        [
            shape((tokens, HD), bf16),
            shape((tokens, HD), bf16),
            shape((LINES, tokens), f32),
            shape((chips + 1, 4 * page_len, HD), bf16),
            shape((8, HD), f32),
        ],
        [SMEM, VMEM, VMEM],
        table,
        table,
        pages,
    )
    parts, gain_rows = call(
        attention,
        "attention",
        [shape((chips, 3, 4, HD), bf16), shape((kvp, HD), f32)],
        [VMEM] * 4,
        gathered,
        keys,
        values,
        member,
    )
    parts = exchange(parts, "kvp", same_core)
    piece = call(
        merge,
        "merge",
        shape((chips, 4 * page_len + 8, HD), bf16),
        [VMEM] * 2,
        parts,
        ordered,
    )
    arrived = exchange(piece, "kvp", same_core)
    attended = lax.all_gather(
        arrived[:, 4 * page_len :], "kvp", axis_index_groups=same_chip
    )
    partial = call(
        project,
        "project",
        shape((2 * tp, 8, HD), bf16),
        [VMEM] * 3,
        attended,
        out_proj,
        packed,
    )
    summands = exchange(partial, ("kvp", "tp"), chip_line)
    own, block = call(
        add_up,
        "add_up",
        [shape((8, HD), f32), shape((chips, 16, HD), bf16)],
        [VMEM],
        summands,
    )
    columns = exchange(block, "kvp", same_core)
    lifted, stream, regrouped = call(
        feed_forward,
        "feed_forward",
        [
            shape((tp, BATCH, HD), bf16),
            shape(residual.shape, bf16),
            shape((chips, 4 * page_len, HD), bf16),
        ],
        [VMEM] * 6,
        columns,
        gain_rows,
        gate_weight,
        up_weight,
        own,
        arrived,
        out_specs=[VMEM, HBM, HBM],
        scratch=[pltpu.VMEM(residual.shape, bf16), pltpu.SemaphoreType.DMA((2,))],
    )
    lifted = exchange(lifted, "tp")
    hidden = call(
        activate, "activate", shape((BATCH, gate_weight.shape[2] // tp), bf16), [VMEM], lifted
    )
    return regrouped.reshape(kv_cache.shape), stream, hidden


def solution(mesh):
    return jax.shard_map(
        shards,
        mesh=mesh,
        in_specs=(
            P(None, None, "tp", "kvp"),
            P(None, None, None, "tp", "kvp"),
            P("kvp", None, None, "tp"),
            P(),
            P(),
            P(None, ("kvp", "tp")),
            P("tp", "kvp"),
            P(("kvp", "tp")),
            P(None, "tp", "kvp"),
            P(None, "tp", "kvp"),
        ),
        out_specs=(P("kvp", None, None, "tp"), P(None, ("kvp", "tp")), P(None, ("kvp", "tp"))),
        check_vma=False,
    )
```

```python
import jax
import jax.numpy as jnp
from jax import lax
from jax.experimental import pallas as pl
from jax.experimental.pallas import tpu as pltpu
from jax.sharding import PartitionSpec as P

D = 16384
HEADS = 128
KVH = 8
HD = 128
STEPS = 2
ROWS = 16
BATCH = STEPS * ROWS
LINES = 4 * ROWS
UNROLL = 64

negative = -1e30
epsilon = 1e-05
bf16 = jnp.bfloat16
f32 = jnp.float32
VMEM = pl.BlockSpec(memory_space=pltpu.VMEM)
SMEM = pl.BlockSpec(memory_space=pltpu.SMEM)
MIB = 1024 * 1024
ALL = 60 * MIB
HBM = pl.BlockSpec(memory_space=pltpu.HBM)


def call(body, name, out_shape, in_specs, *args, out_specs=None, scratch=(), room=16 * MIB):
    if out_specs is None:
        out_specs = [VMEM] * len(out_shape) if isinstance(out_shape, list) else VMEM
    return pl.pallas_call(
        body,
        out_shape=out_shape,
        in_specs=in_specs,
        out_specs=out_specs,
        scratch_shapes=scratch,
        compiler_params=pltpu.CompilerParams(vmem_limit_bytes=room),
        name=name,
    )(*args)


def pack_inputs(*refs):
    sources, (out, table), targets, done = refs[:6], refs[6:8], refs[8:14], refs[14]
    queries, fresh, gain, residual, owner, context = targets
    copies = [
        pltpu.make_async_copy(source, target, done.at[k])
        for k, (source, target) in enumerate(zip(sources, targets))
    ]
    for copy in copies:
        copy.start()
    for copy in copies:
        copy.wait()
    heads = queries.shape[3]
    rows = queries[...].astype(f32).reshape(2 * BATCH, heads).astype(bf16)
    entry = lax.broadcasted_iota(jnp.int32, (2 * BATCH, heads * BATCH), 0)
    target = lax.broadcasted_iota(jnp.int32, (2 * BATCH, heads * BATCH), 1)
    head = lax.broadcasted_iota(jnp.int32, (heads, heads * BATCH), 0)
    lane = lax.broadcasted_iota(jnp.int32, (heads, heads * BATCH), 1)
    lines = []
    for d in range(2):
        place = (entry % 2 == d) & (entry // 2 == target % BATCH)
        spread = lax.dot_general(
            rows,
            jnp.where(place, 1.0, 0.0).astype(bf16),
            (((0,), (0,)), ((), ())),
            preferred_element_type=f32,
        )
        lines.append(
            jnp.sum(jnp.where(lane // BATCH == head, spread, 0.0), axis=0, keepdims=True)
        )
    q = jnp.concatenate(lines, axis=0)
    new = fresh[...].astype(f32)
    kv = [new[u, w] for w in range(2) for u in range(STEPS)]
    g = gain[...].astype(f32)
    g = jnp.concatenate([g, g], axis=1)
    tail = kv + [jnp.concatenate([g, g], axis=0)]
    half = q.shape[1] // 2
    lines = [
        jnp.concatenate([q[:, c * half : c * half + half]] + tail, axis=1).astype(bf16)
        for c in range(2)
    ]
    sent = jnp.stack(lines, axis=0)[None]
    out[...] = jnp.broadcast_to(sent, (out.shape[0] // 2,) + sent.shape[1:]).reshape(out.shape)
    me = lax.axis_index("kvp")
    line = lax.broadcasted_iota(jnp.int32, owner.shape, 0)
    to = jnp.sum(jnp.where(line == me // 2, owner[...], 0), axis=0, keepdims=True)
    place = jnp.where((to ^ me) & 1 == 0, to >> 1, owner.shape[0])
    spans = jnp.concatenate(
        [context[...], jnp.zeros((1, HD - context.shape[1]), jnp.int32)], axis=1
    )
    table[...] = jnp.concatenate(
        [
            pack(residual[...].astype(f32)),
            place.astype(f32),
            spans.astype(f32),
            jnp.zeros((6, HD), f32),
        ],
        axis=0,
    )


def prepare(
    numbers, table, pages, keys, values, member, ordered, packed
):
    me = lax.axis_index("kvp")
    count, page_len = pages.shape[1], pages.shape[3]
    half = count * page_len
    for c in range(2):
        cache = pages[c].astype(f32)
        keys[c * half : c * half + half] = cache[:, 0].reshape(-1, HD).astype(bf16)
        values[c * half : c * half + half] = cache[:, 1].reshape(-1, HD).astype(bf16)
    page = lax.broadcasted_iota(jnp.int32, (8, member.shape[1]), 1) // page_len
    page = page + me // 2 * 2 * count
    row = jnp.zeros(page.shape, jnp.int32)
    end = jnp.int32(0)
    for r in range(ROWS - 1):
        end = end + numbers[9, r].astype(jnp.int32)
        row = row + (page >= end).astype(jnp.int32)
    line = lax.broadcasted_iota(jnp.int32, member.shape, 0) % ROWS
    member[...] = jnp.where(row[:1] == line, 1.0, 0.0)
    packed[...] = table[:8]


    def one(c, carry):
        for core in range(2):
            place = numbers[8, core * count + c].astype(jnp.int32)
            ordered[place, core * 2 * page_len : (core + 1) * 2 * page_len] = pages[
                core, c
            ].reshape(2 * page_len, HD)
        return carry

    lax.fori_loop(0, count, one, 0, unroll=UNROLL)


def attention(gathered, key_ref, value_ref, member_ref, out, gain_out):
    turned = gathered[...].astype(f32).reshape(HD, -1).T
    combos = HEADS // KVH // 2 * BATCH
    q = turned[:combos].astype(bf16)
    fresh = turned[combos:].astype(bf16)
    fresh_k, fresh_v = fresh[:BATCH], fresh[BATCH : 2 * BATCH]
    keys, values = key_ref[...], value_ref[...]
    tokens = keys.shape[0]
    peers = out.shape[0]
    tail = gathered[...].astype(f32).reshape(HD, -1)[:, combos + 2 * BATCH :].astype(bf16)
    take = lax.broadcasted_iota(jnp.int32, (HD // 2, HD), 1) - 2 * lax.broadcasted_iota(
        jnp.int32, (HD // 2, HD), 0
    )
    gain_out[...] = jnp.concatenate(
        [
            jnp.dot(
                jnp.where(take == k, 1.0, 0.0).astype(bf16), tail, preferred_element_type=f32
            )
            for k in range(2)
        ],
        axis=1,
    )
    me = lax.axis_index("kvp")
    scale = HD ** (-0.5)
    nt = (((1,), (1,)), ((), ()))
    scores = lax.dot_general(q, keys, nt, preferred_element_type=f32) * scale
    fresh_scores = lax.dot_general(q, fresh_k, nt, preferred_element_type=f32) * scale

    combo = lax.broadcasted_iota(jnp.int32, (combos, 1), 0)
    combo_row = combo % ROWS
    combo_step = (combo // ROWS) % STEPS
    lines = member_ref.shape[0]
    member = jnp.broadcast_to(member_ref[...][None], (combos // lines, lines, tokens))
    member = member.reshape(combos, tokens) > 0.5
    entry = lax.broadcasted_iota(jnp.int32, (1, BATCH), 1)
    fresh_member = (
        (combo_row == entry % ROWS) & (entry // ROWS <= combo_step) & (me // 2 == 0)
    )
    scores = jnp.where(member, scores, negative)
    fresh_scores = jnp.where(fresh_member, fresh_scores, negative)
    peak = jnp.maximum(
        jnp.max(scores, axis=1, keepdims=True), jnp.max(fresh_scores, axis=1, keepdims=True)
    )
    peak = peak.astype(bf16).astype(f32)
    weights = jnp.where(member, jnp.exp(scores - peak), 0.0)
    fresh_weights = jnp.where(fresh_member, jnp.exp(fresh_scores - peak), 0.0)
    total = jnp.sum(weights, axis=1, keepdims=True) + jnp.sum(
        fresh_weights, axis=1, keepdims=True
    )
    numerator = jnp.dot(
        weights.astype(bf16), values, preferred_element_type=f32
    ) + jnp.dot(fresh_weights.astype(bf16), fresh_v, preferred_element_type=f32)
    high = total.astype(bf16).astype(f32)
    columns = [x.reshape(peers, 8, 1) for x in (peak, high, total - high)]
    lane = lax.broadcasted_iota(jnp.int32, (peers, 4, HD), 2)
    stats = jnp.zeros((peers, 4, HD), f32)
    for k in range(5, -1, -1):
        column = columns[k % 3][:, :4] if k < 3 else columns[k % 3][:, 4:]
        stats = jnp.where(lane < 16 * k + 16, column, stats)
    numerator = numerator.reshape(peers, 8, HD)
    out[:, 0] = numerator[:, :4].astype(bf16)
    out[:, 1] = numerator[:, 4:].astype(bf16)
    out[:, 2] = stats.astype(bf16)


def merge(parts, ordered, out):
    stats = parts[:, 2].astype(f32)
    values = []
    for half in range(2):
        at = 48 * half
        peak = stats[:, :, at : at + 1]
        total = stats[:, :, at + 16 : at + 17] + stats[:, :, at + 32 : at + 33]
        factor = jnp.exp(peak - jnp.max(peak, axis=0, keepdims=True))
        numerator = jnp.sum(factor * parts[:, half].astype(f32), axis=0)
        values.append(numerator / jnp.sum(factor * total, axis=0))
    value = jnp.concatenate(values, axis=0).astype(bf16)
    value = jnp.broadcast_to(value[None], (out.shape[0],) + value.shape)
    out[...] = jnp.concatenate([ordered[: out.shape[0], :16], value], axis=1)


def pack(x):
    return jnp.concatenate([x[8 * q : 8 * q + 8] for q in range(4)], axis=1)


def project(attended, weight, residual, out):
    x = attended[...].astype(f32).reshape(-1, BATCH, HD).astype(bf16)
    flat = jnp.concatenate([x[h] for h in range(x.shape[0])], axis=1)
    acc = jnp.dot(flat, weight[...], preferred_element_type=f32)
    tp = out.shape[0] // 2
    me = lax.axis_index("tp")
    blocks = [
        pack(acc[:, 32 * j : 32 * j + 32]) + jnp.where(me == j, residual[...], 0.0)
        for j in range(tp)
    ]
    out[...] = jnp.stack(blocks * 2, axis=0).astype(bf16)


def add_up(parts, ordered, own, sent):
    total = jnp.sum(parts[...].astype(f32).reshape(2, -1, 8, HD), axis=1)
    value = total.reshape(16, HD).astype(bf16)
    wide = value.astype(f32)
    own[...] = jnp.where(lax.axis_index("kvp") % 2 == 0, wide[:8], wide[8:])
    value = jnp.broadcast_to(value[None], (sent.shape[0],) + value.shape)
    sent[...] = jnp.concatenate([value, ordered[: sent.shape[0], 16:]], axis=1)


def feed_forward(
    columns, gain, gate_weight, up_weight, own, pages, out, stream, regrouped, staged, done
):
    wide = own[...]
    staged[...] = jnp.concatenate(
        [wide[:, 32 * q : 32 * q + 32] for q in range(4)], axis=0
    ).astype(bf16)
    copies = [
        pltpu.make_async_copy(pages.at[:, :16], regrouped.at[:, :16], done.at[0]),
        pltpu.make_async_copy(columns.at[:, 16:], regrouped.at[:, 16:], done.at[2]),
        pltpu.make_async_copy(staged, stream, done.at[1]),
    ]
    for copy in copies:
        copy.start()
    x = columns[:, :16].astype(f32).reshape(-1, 8, HD)
    square = jnp.sum(x * x, axis=0)
    square = jnp.concatenate(
        [jnp.sum(square[:, 32 * q : 32 * q + 32], axis=1, keepdims=True) for q in range(4)],
        axis=0,
    )
    scaled = (x * gain[...][:, None, :]).reshape(-1, 4, 8, HD)
    lane = lax.broadcasted_iota(jnp.int32, (scaled.shape[0], 8, HD), 2) // 32
    blocks = []
    for q in range(4):
        block = None
        for t in range(4):
            piece = scaled[:, t]
            if t != q:
                piece = pltpu.roll(piece, (t - q) * 32 % HD, 2)
            block = piece if block is None else jnp.where(lane == t, piece, block)
        blocks.append(block)
    rows = jnp.concatenate(blocks, axis=1).astype(bf16)
    flat = jnp.concatenate([rows[g] for g in range(rows.shape[0])], axis=1)
    width = gate_weight.shape[2]
    gate = jnp.dot(flat, gate_weight[...].reshape(-1, width), preferred_element_type=f32)
    up = jnp.dot(flat, up_weight[...].reshape(-1, width), preferred_element_type=f32)
    peers = out.shape[0]
    part = width // peers
    high = square.astype(bf16).astype(f32)
    tail = lax.broadcasted_iota(jnp.int32, (BATCH, 64 - part), 1)
    tail = jnp.where(tail == 0, high, jnp.where(tail == 1, square - high, 0.0))
    gap = jnp.zeros((BATCH, 64 - part), f32)
    for j in range(peers):
        out[j] = jnp.concatenate(
            [
                gate[:, part * j : part * j + part],
                gap,
                up[:, part * j : part * j + part],
                tail,
            ],
            axis=1,
        ).astype(bf16)
    for copy in copies:
        copy.wait()


def activate(parts, out):
    total = jnp.sum(parts[...].astype(f32), axis=0)
    part = out.shape[1]
    square = total[:, 64 + part : 65 + part] + total[:, 65 + part : 66 + part]
    inverse = lax.rsqrt(square / D + epsilon)
    gated = total[:, :part] * inverse
    lifted = total[:, 64 : 64 + part] * inverse
    out[...] = (gated / (1.0 + jnp.exp(-gated)) * lifted).astype(bf16)


def exchange(x, axis, groups=None):
    return lax.all_to_all(
        x, axis, split_axis=0, concat_axis=0, tiled=True, axis_index_groups=groups
    )


def shards(
    queries,
    fresh_kv,
    kv_cache,
    page_owner,
    context_pages,
    residual,
    out_proj,
    norm_gain,
    gate_weight,
    up_weight,
):
    kvp = lax.axis_size("kvp")
    tp = lax.axis_size("tp")
    shape = jax.ShapeDtypeStruct
    combos = queries.shape[2] * BATCH

    count, page_len = kv_cache.shape[0], kv_cache.shape[2]
    tokens = 2 * count * page_len
    raw = (
        queries.transpose(0, 1, 3, 2),
        fresh_kv[:, :, :, 0].transpose(0, 2, 3, 1),
        norm_gain.reshape(1, -1),
        residual,
        page_owner.reshape(-1, HD),
        context_pages.reshape(1, -1),
    )
    sent, table = call(
        pack_inputs,
        "pack_inputs",
        [shape((kvp, 2, combos // 2 + 4 * BATCH), bf16), shape((16, HD), f32)],
        [HBM] * 6,
        *raw,
        scratch=[pltpu.VMEM(x.shape, x.dtype) for x in raw] + [pltpu.SemaphoreType.DMA((6,))],
        room=ALL,
    )
    gathered = exchange(sent, "kvp")
    chips = kvp // 2
    chip_line = [[chip * 2 * tp + k for k in range(2 * tp)] for chip in range(chips)]
    same_core = [[2 * chip + core for chip in range(chips)] for core in range(2)]
    same_chip = [[2 * chip, 2 * chip + 1] for chip in range(chips)]
    pages = lax.all_gather(kv_cache, "kvp", axis_index_groups=same_chip)
    keys, values, member, ordered, packed = call(
        prepare,
        "prepare",
        [
            shape((tokens, HD), bf16),
            shape((tokens, HD), bf16),
            shape((LINES, tokens), f32),
            shape((chips + 1, 4 * page_len, HD), bf16),
            shape((8, HD), f32),
        ],
        [SMEM, VMEM, VMEM],
        table,
        table,
        pages,
    )
    parts, gain_rows = call(
        attention,
        "attention",
        [shape((chips, 3, 4, HD), bf16), shape((kvp, HD), f32)],
        [VMEM] * 4,
        gathered,
        keys,
        values,
        member,
    )
    parts = exchange(parts, "kvp", same_core)
    piece = call(
        merge,
        "merge",
        shape((chips, 2 * page_len + 8, HD), bf16),
        [VMEM] * 2,
        parts,
        ordered,
    )
    arrived = exchange(piece, "kvp", same_core)
    attended = lax.all_gather(
        arrived[:, 2 * page_len :], "kvp", axis_index_groups=same_chip
    )
    partial = call(
        project,
        "project",
        shape((2 * tp, 8, HD), bf16),
        [VMEM] * 3,
        attended,
        out_proj,
        packed,
    )
    summands = exchange(partial, ("kvp", "tp"), chip_line)
    own, block = call(
        add_up,
        "add_up",
        [shape((8, HD), f32), shape((chips, 16 + 2 * page_len, HD), bf16)],
        [VMEM] * 2,
        summands,
        ordered,
    )
    columns = exchange(block, "kvp", same_core)
    lifted, stream, regrouped = call(
        feed_forward,
        "feed_forward",
        [
            shape((tp, BATCH, HD), bf16),
            shape(residual.shape, bf16),
            shape((chips, 4 * page_len, HD), bf16),
        ],
        [VMEM] * 6,
        columns,
        gain_rows,
        gate_weight,
        up_weight,
        own,
        arrived,
        out_specs=[VMEM, HBM, HBM],
        scratch=[pltpu.VMEM(residual.shape, bf16), pltpu.SemaphoreType.DMA((3,))],
    )
    lifted = exchange(lifted, "tp")
    hidden = call(
        activate, "activate", shape((BATCH, gate_weight.shape[2] // tp), bf16), [VMEM], lifted
    )
    return regrouped.reshape(kv_cache.shape), stream, hidden


def solution(mesh):
    return jax.shard_map(
        shards,
        mesh=mesh,
        in_specs=(
            P(None, None, "tp", "kvp"),
            P(None, None, None, "tp", "kvp"),
            P("kvp", None, None, "tp"),
            P(),
            P(),
            P(None, ("kvp", "tp")),
            P("tp", "kvp"),
            P(("kvp", "tp")),
            P(None, "tp", "kvp"),
            P(None, "tp", "kvp"),
        ),
        out_specs=(P("kvp", None, None, "tp"), P(None, ("kvp", "tp")), P(None, ("kvp", "tp"))),
        check_vma=False,
    )
```
